32 devices in a mesh: row: 8 (over y, x, core), col: 4 (over z).
Axes of the slice: x: 2, y: 2, z: 4, core: 2. Of those that a mesh axis runs over, the one named last changes fastest.
Arguments:
- tokens: bfloat16 [64, 8192], P('row', 'col'), may hold values from -6 to 6
- gate_weight: bfloat16 [8192, 24576], P('col', 'row'), may hold values from -0.0625 to 0.0625
- up_weight: bfloat16 [8192, 24576], P('col', 'row'), may hold values from -0.0625 to 0.0625
- down_weight: bfloat16 [24576, 8192], P('row', 'col'), may hold values from -0.0390625 to 0.0390625
- out_grad: bfloat16 [64, 8192], P('row', 'col'), may hold values from -1.5 to 1.5
Outputs:
- mixed: bfloat16 [64, 8192], P('row', 'col')
- input_grad: bfloat16 [64, 8192], P('row', 'col')
- gate_grad: bfloat16 [8192, 24576], P('col', 'row')
- up_grad: bfloat16 [8192, 24576], P('col', 'row')
- down_grad: bfloat16 [24576, 8192], P('row', 'col')
The draws below stay inside these ranges and needn't reach their ends.
All inputs are finite; a program needn't handle non-finite values.
Results may differ from the reference program's by a relative error of at most 0.0049.
Values may be sent and summed in bfloat16 or wider, within the bound.
No kernel may reach another device: no remote copies, remote signals or barrier semaphores. Data moves between devices by JAX's collectives and lax.ppermute only.
A program may use at most 192 MiB of HBM per device.

```python
import jax
import jax.numpy as jnp
from jax import lax

D = 8192
FF = 24576
TOKENS = 64


def level_of(key, dims, pieces, least, high):
    loudness = 1.0
    for dim, blocks in pieces:
        draws = jax.random.uniform(jax.random.fold_in(jax.random.fold_in(key, 6), dim), (blocks,), jnp.float32, least / len(pieces), high / len(pieces))
        loudness = loudness * jnp.repeat(jnp.exp(draws), dims[dim] // blocks).reshape((-1,) + (1,) * (len(dims) - 1 - dim))
    return loudness


def noise(key, extent, spread, most, split=(), kind=jnp.bfloat16):
    factor_of = level_of(key, extent, split, -0.22, 0.18) if split else 1.0
    entries = jax.random.normal(key, extent, jnp.float32) * spread * factor_of
    return jnp.minimum(jnp.maximum(entries, -most), most).astype(kind)


def setup_inputs(seed: int = 0) -> dict:
    streams_of = jax.random.split(jax.random.key(seed), 6)
    tokens = noise(streams_of[0], (TOKENS, D), 1.0, 6.0, ((0, 8), (1, 4)))
    gate_weight = noise(streams_of[1], (D, FF), D ** -0.5, 0.0625, ((0, 4), (1, 8)))
    up_weight = noise(streams_of[2], (D, FF), D ** -0.5, 0.0625, ((0, 4), (1, 8)))
    down_weight = noise(streams_of[3], (FF, D), FF ** -0.5, 0.0390625, ((0, 8), (1, 4)))
    out_grad = noise(streams_of[4], (TOKENS, D), 0.25, 1.5, ((0, 8), (1, 4)))
    return dict(tokens=tokens, gate_weight=gate_weight, up_weight=up_weight, down_weight=down_weight, out_grad=out_grad)


def reference(tokens, gate_weight, up_weight, down_weight, out_grad):
    back = (((1,), (1,)), ((), ()))
    contract = (((0,), (0,)), ((), ()))
    gate = jnp.dot(tokens, gate_weight, preferred_element_type=jnp.float32)
    up = jnp.dot(tokens, up_weight, preferred_element_type=jnp.float32)
    hidden_grad = lax.dot_general(out_grad, down_weight, back, preferred_element_type=jnp.float32)
    sigmoid = jax.nn.sigmoid(gate)
    swish = gate * sigmoid
    hidden = (swish * up).astype(jnp.bfloat16)
    down_grad = lax.dot_general(hidden, out_grad, contract, preferred_element_type=jnp.float32).astype(jnp.bfloat16)
    gate_delta = (hidden_grad * up * sigmoid * (1.0 + gate * (1.0 - sigmoid))).astype(jnp.bfloat16)
    up_delta = (hidden_grad * swish).astype(jnp.bfloat16)
    gate_grad = lax.dot_general(tokens, gate_delta, contract, preferred_element_type=jnp.float32).astype(jnp.bfloat16)
    up_grad = lax.dot_general(tokens, up_delta, contract, preferred_element_type=jnp.float32).astype(jnp.bfloat16)
    mixed = jnp.dot(hidden, down_weight, preferred_element_type=jnp.float32)
    input_grad = lax.dot_general(gate_delta, gate_weight, back, preferred_element_type=jnp.float32)
    input_grad = input_grad + lax.dot_general(up_delta, up_weight, back, preferred_element_type=jnp.float32)
    return mixed.astype(jnp.bfloat16), input_grad.astype(jnp.bfloat16), gate_grad, up_grad, down_grad
```

```python
import functools

import jax
import jax.numpy as jnp
from jax import lax
from jax.experimental import pallas as pl
from jax.experimental.pallas import tpu as pltpu
from jax.sharding import PartitionSpec as P

BF16 = jnp.bfloat16
F32 = jnp.float32
VMEM_LIMIT = 48 * 1024 * 1024
BACK = (((1,), (1,)), ((), ()))
CONTRACT = (((0,), (0,)), ((), ()))


def dot(a, b):
    return jnp.dot(a, b, preferred_element_type=F32)


def swap(x, axis, size, k):
    return lax.ppermute(x, axis, [(i, i ^ k) for i in range(size)])


def estimate(flops, num_bytes):
    return pl.CostEstimate(flops=flops, bytes_accessed=num_bytes, transcendentals=0)


def assemble_kernel(rows, *refs):
    pieces, (tok, grad, tok_t, grad_t) = refs[:-4], refs[-4:]
    both = [p[...].astype(F32) for p in pieces]
    all_tok = jnp.concatenate([b[:rows] for b in both], axis=0)
    all_grad = jnp.concatenate([b[rows:] for b in both], axis=0)
    tok[...] = all_tok.astype(BF16)
    grad[...] = all_grad.astype(BF16)
    tok_t[...] = all_tok.T.astype(BF16)
    grad_t[...] = all_grad.T.astype(BF16)


def assemble(pieces, rows):
    total, width = rows * len(pieces), pieces[0].shape[1]
    flat, turned = (total, width), (width, total)
    return pl.pallas_call(
        functools.partial(assemble_kernel, rows),
        out_shape=[jax.ShapeDtypeStruct(s, BF16) for s in (flat, flat, turned, turned)],
        compiler_params=pltpu.CompilerParams(vmem_limit_bytes=VMEM_LIMIT),
        cost_estimate=estimate(0, 12 * total * width),
        name="assemble",
    )(*pieces)


def sums_kernel(where, tok, grad_t, gate_w, up_w, down_w, out):
    out[0] = dot(tok[...], gate_w[...]).astype(out.dtype)
    out[1] = dot(tok[...], up_w[...]).astype(out.dtype)
    out[2] = dot(down_w[...], grad_t[...]).T.astype(out.dtype)


def partial_sums(where, tok, grad_t, gate_w, up_w, down_w, units, block, dtype):
    total, width = tok.shape
    steps = units // block
    return pl.pallas_call(
        sums_kernel,
        grid_spec=pltpu.PrefetchScalarGridSpec(
            num_scalar_prefetch=1,
            grid=(steps,),
            in_specs=[
                pl.BlockSpec((total, width), lambda i, w: (0, 0)),
                pl.BlockSpec((width, total), lambda i, w: (0, 0)),
                pl.BlockSpec((width, block), lambda i, w: (0, w[0] * steps + i)),
                pl.BlockSpec((width, block), lambda i, w: (0, w[0] * steps + i)),
                pl.BlockSpec((block, width), lambda i, w: (w[0] * steps + i, 0)),
            ],
            out_specs=pl.BlockSpec((3, total, block), lambda i, w: (0, 0, i)),
        ),
        out_shape=jax.ShapeDtypeStruct((3, total, units), dtype),
        compiler_params=pltpu.CompilerParams(vmem_limit_bytes=VMEM_LIMIT),
        cost_estimate=estimate(6 * total * width * units, 6 * width * units),
        name="partial_sums",
    )(where, tok, grad_t, gate_w, up_w, down_w)


def activate_kernel(own, *refs):
    others, out = refs[:-1], refs[-1]
    gate, up, hidden_grad = (
        functools.reduce(lambda s, o: s + o[j].astype(F32), others, own[j]) for j in range(3)
    )
    sig = jax.nn.sigmoid(gate)
    swish = gate * sig
    out[0] = (swish * up).astype(BF16)
    out[1] = (hidden_grad * up * sig * (1.0 + gate * (1.0 - sig))).astype(BF16)
    out[2] = (hidden_grad * swish).astype(BF16)


def activate(own, others):
    size = own.size
    return pl.pallas_call(
        activate_kernel,
        out_shape=jax.ShapeDtypeStruct(own.shape, BF16),
        compiler_params=pltpu.CompilerParams(vmem_limit_bytes=VMEM_LIMIT),
        cost_estimate=estimate(8 * size, 12 * size),
        name="activate",
    )(own, *others)


def products_kernel(first, where, act, gate_w, up_w, down_w, *refs):
    before, (mixed, back, back_t) = refs[:2], refs[-3:]
    step = pl.program_id(0)

    @pl.when(step == 0)
    def _():
        mixed[...] = jnp.zeros_like(mixed) if first else before[0][...]
        back_t[...] = jnp.zeros_like(back_t)

    gate_delta = act[1].astype(F32).T.astype(BF16)
    up_delta = act[2].astype(F32).T.astype(BF16)
    mixed[...] += dot(act[0], down_w[...])
    back_t[...] += dot(gate_w[...], gate_delta) + dot(up_w[...], up_delta)

    @pl.when(step == pl.num_programs(0) - 1)
    def _():
        turned = back_t[...].T
        back[...] = turned if first else before[1][...] + turned


def products(where, act, gate_w, up_w, down_w, before, after, block):
    _, total, units = act.shape
    width = gate_w.shape[0]
    steps = units // block
    whole = pl.BlockSpec((total, width), lambda i, w: (0, 0))
    return pl.pallas_call(
        functools.partial(products_kernel, not before),
        grid_spec=pltpu.PrefetchScalarGridSpec(
            num_scalar_prefetch=1,
            grid=(steps,),
            in_specs=[
                pl.BlockSpec((3, total, block), lambda i, w: (0, 0, i)),
                pl.BlockSpec((width, block), lambda i, w: (0, w[0] * steps + i)),
                pl.BlockSpec((width, block), lambda i, w: (0, w[0] * steps + i)),
                pl.BlockSpec((block, width), lambda i, w: (w[0] * steps + i, 0)),
            ]
            + [whole] * len(before)
            + [pl.BlockSpec(memory_space=pl.ANY)] * len(after),
            out_specs=[whole, whole],
            scratch_shapes=[pltpu.VMEM((width, total), F32)],
        ),
        out_shape=[jax.ShapeDtypeStruct((total, width), F32)] * 2,
        compiler_params=pltpu.CompilerParams(vmem_limit_bytes=VMEM_LIMIT),
        cost_estimate=estimate(6 * total * width * units, 6 * width * units),
        name="products",
    )(where, act, gate_w, up_w, down_w, *before, *after)


def grads_kernel(where, act, tok_t, grad, *refs):
    gate_g, up_g, down_g = refs[-3:]
    gate_g[...] = dot(tok_t[...], act[1]).astype(BF16)
    up_g[...] = dot(tok_t[...], act[2]).astype(BF16)
    down_g[...] = dot(act[0].astype(F32).T.astype(BF16), grad[...]).astype(BF16)


def weight_grads(where, act, tok_t, grad, before, after, all_units, block):
    _, total, units = act.shape
    width = grad.shape[1]
    steps = units // block
    hold = [pl.BlockSpec(memory_space=pl.ANY)]
    extra = list(before) + list(after)
    return pl.pallas_call(
        grads_kernel,
        grid_spec=pltpu.PrefetchScalarGridSpec(
            num_scalar_prefetch=1,
            grid=(steps,),
            in_specs=[
                pl.BlockSpec((3, total, block), lambda i, w: (0, 0, i)),
                pl.BlockSpec((width, total), lambda i, w: (0, 0)),
                pl.BlockSpec((total, width), lambda i, w: (0, 0)),
            ]
            + hold * len(extra),
            out_specs=[
                pl.BlockSpec((width, block), lambda i, w: (0, w[0] * steps + i)),
                pl.BlockSpec((width, block), lambda i, w: (0, w[0] * steps + i)),
                pl.BlockSpec((block, width), lambda i, w: (w[0] * steps + i, 0)),
            ],
        ),
        out_shape=[
            jax.ShapeDtypeStruct((width, all_units), BF16),
            jax.ShapeDtypeStruct((width, all_units), BF16),
            jax.ShapeDtypeStruct((all_units, width), BF16),
        ],
        input_output_aliases={4 + i: i for i in range(len(before))},
        compiler_params=pltpu.CompilerParams(vmem_limit_bytes=VMEM_LIMIT),
        cost_estimate=estimate(6 * total * width * units, 6 * width * units),
        name="weight_grads",
    )(where, act, tok_t, grad, *extra)


def pairwise(n_row, n_col, tokens, gate_weight, up_weight, down_weight, out_grad):
    rows, width = tokens.shape
    all_units = gate_weight.shape[1]
    units = all_units // n_col
    block = 256
    col = lax.axis_index("col")

    mine = jnp.concatenate([tokens, out_grad], axis=0)
    even = [mine] + [swap(mine, "row", n_row, k) for k in range(2, n_row, 2)]
    odd = [swap(piece, "row", n_row, 1) for piece in even]
    order = list(range(0, n_row, 2)) + list(range(1, n_row, 2))
    tok, grad, tok_t, grad_t = assemble(even + odd, rows)

    far_first = sorted(range(1, n_col), reverse=True)
    where = {k: jnp.bitwise_xor(col, k).reshape(1) for k in range(n_col)}

    def sums_of(k, dtype):
        return partial_sums(
            where[k], tok, grad_t, gate_weight, up_weight, down_weight, units, block, dtype
        )

    arrived = [swap(sums_of(k, BF16), "col", n_col, k) for k in far_first]
    own = activate(sums_of(0, F32), arrived)

    acts = {0: own}
    for k in (1 << b for b in range(n_col.bit_length() - 1)):
        acts[k] = swap(own, "col", n_col, k)
    terms, grads, late = (), (), []
    for k in range(n_col):
        terms = products(
            where[k], acts[k], gate_weight, up_weight, down_weight, terms, grads, block
        )
        if k < n_col // 2:
            grads = weight_grads(where[k], acts[k], tok_t, grad, grads, (), all_units, block)
        else:
            late.append(k)
        if k == 0:
            for j in range(n_col):
                if j not in acts:
                    low = j & -j
                    held, _ = lax.optimization_barrier((acts[j ^ low], (terms, grads)))
                    acts[j] = swap(held, "col", n_col, low)
    both = jnp.stack(terms).reshape(2, n_row, rows, width)
    sent = both.astype(BF16)
    parts = [
        swap(sent[:, i], "row", n_row, k).astype(F32) for i, k in enumerate(order) if k
    ]
    for k in late:
        grads = weight_grads(where[k], acts[k], tok_t, grad, grads, terms, all_units, block)
    mixed, input_grad = functools.reduce(jnp.add, parts, both[:, 0]).astype(BF16)
    return (mixed, input_grad, *grads)


def gathered(tokens, gate_weight, up_weight, down_weight, out_grad):
    tok = lax.all_gather(tokens, "row", axis=0, tiled=True)
    grad = lax.all_gather(out_grad, "row", axis=0, tiled=True)

    def total(x):
        return lax.psum_scatter(x, "col", scatter_dimension=0, tiled=True)

    def back_dot(a, b):
        return lax.dot_general(a, b, BACK, preferred_element_type=F32)

    def outer(a, b):
        return lax.dot_general(a, b, CONTRACT, preferred_element_type=F32).astype(BF16)

    gate, up = total(dot(tok, gate_weight)), total(dot(tok, up_weight))
    hidden_grad = total(back_dot(grad, down_weight))
    sig = jax.nn.sigmoid(gate)
    swish = gate * sig
    hidden = (swish * up).astype(BF16)
    gate_delta = (hidden_grad * up * sig * (1.0 + gate * (1.0 - sig))).astype(BF16)
    up_delta = (hidden_grad * swish).astype(BF16)
    hidden, gate_delta, up_delta = (
        lax.all_gather(x, "col", axis=0, tiled=True) for x in (hidden, gate_delta, up_delta)
    )
    mixed = dot(hidden, down_weight)
    input_grad = back_dot(gate_delta, gate_weight) + back_dot(up_delta, up_weight)
    mixed, input_grad = (
        lax.psum_scatter(x, "row", scatter_dimension=0, tiled=True).astype(BF16)
        for x in (mixed, input_grad)
    )
    return (
        mixed,
        input_grad,
        outer(tok, gate_delta),
        outer(tok, up_delta),
        outer(hidden, grad),
    )


def solution(mesh):
    n_row, n_col = mesh.shape["row"], mesh.shape["col"]

    def shards(*args):
        tokens, gate_weight = args[:2]
        fits = (
            n_row & (n_row - 1) == 0
            and n_col & (n_col - 1) == 0
            and n_row > 1
            and n_col > 1
            and tokens.shape[0] % 8 == 0
            and tokens.shape[1] % 128 == 0
            and gate_weight.shape[1] % (256 * n_col) == 0
        )
        if fits:
            return pairwise(n_row, n_col, *args)
        return gathered(*args)

    return jax.shard_map(
        shards,
        mesh=mesh,
        in_specs=(
            P("row", "col"),
            P("col", "row"),
            P("col", "row"),
            P("row", "col"),
            P("row", "col"),
        ),
        out_specs=(
            P("row", "col"),
            P("row", "col"),
            P("col", "row"),
            P("col", "row"),
            P("row", "col"),
        ),
        check_vma=False,
    )
```

```python
import functools

import jax
import jax.numpy as jnp
from jax import lax
from jax.experimental import pallas as pl
from jax.experimental.pallas import tpu as pltpu
from jax.sharding import PartitionSpec as P

BF16 = jnp.bfloat16
F32 = jnp.float32
VMEM_LIMIT = 48 * 1024 * 1024
CHUNK = 256
BACK = (((1,), (1,)), ((), ()))
CONTRACT = (((0,), (0,)), ((), ()))
PARAMS = pltpu.CompilerParams(vmem_limit_bytes=VMEM_LIMIT)
HOLD = pl.BlockSpec(memory_space=pl.ANY)


def dot(a, b):
    return jnp.dot(a, b, preferred_element_type=F32)


def swap(x, axis, size, k):
    return lax.ppermute(x, axis, [(i, i ^ k) for i in range(size)])


def estimate(flops, num_bytes):
    return pl.CostEstimate(flops=flops, bytes_accessed=num_bytes, transcendentals=0)


def array(shape, dtype):
    return jax.ShapeDtypeStruct(shape, dtype)


def pack_kernel(tokens, out_grad, out):
    joined = jnp.concatenate([tokens[...].astype(F32), out_grad[...].astype(F32)], axis=0)
    out[...] = joined.astype(BF16)


def pack(tokens, out_grad):
    rows, width = tokens.shape
    return pl.pallas_call(
        pack_kernel,
        out_shape=array((2 * rows, width), BF16),
        compiler_params=PARAMS,
        cost_estimate=estimate(0, 8 * rows * width),
        name="pack",
    )(tokens, out_grad)


def assemble_kernel(rows, *refs):
    pieces, (tok, grad, tok_t, grad_t) = refs[:-4], refs[-4:]
    both = [p[...].astype(F32) for p in pieces]
    all_tok = jnp.concatenate([b[:rows] for b in both], axis=0)
    all_grad = jnp.concatenate([b[rows:] for b in both], axis=0)
    tok[...] = all_tok.astype(BF16)
    grad[...] = all_grad.astype(BF16)
    tok_t[...] = all_tok.T.astype(BF16)
    grad_t[...] = all_grad.T.astype(BF16)


def assemble(pieces, rows):
    total, width = rows * len(pieces), pieces[0].shape[1]
    flat, turned = (total, width), (width, total)
    return pl.pallas_call(
        functools.partial(assemble_kernel, rows),
        out_shape=[array(shape, BF16) for shape in (flat, flat, turned, turned)],
        compiler_params=PARAMS,
        cost_estimate=estimate(0, 12 * total * width),
        name="assemble",
    )(*pieces)


def weight_specs(units):
    wide = pl.BlockSpec((CHUNK, units), lambda i, w: (i, w[0]))
    tall = pl.BlockSpec((units, CHUNK), lambda i, w: (w[0], i))
    return [wide, wide, tall]


def sums_kernel(where, tok, grad_t, gate_w, up_w, down_w, *refs):
    out, gate, up, back = refs[-4:]
    step = pl.program_id(0)

    @pl.when(step == 0)
    def _():
        for acc in (gate, up, back):
            acc[...] = jnp.zeros_like(acc)

    gate[...] += dot(tok[...], gate_w[...])
    up[...] += dot(tok[...], up_w[...])
    back[...] += dot(down_w[...], grad_t[...])

    @pl.when(step == pl.num_programs(0) - 1)
    def _():
        out[0] = gate[...].astype(out.dtype)
        out[1] = up[...].astype(out.dtype)
        out[2] = back[...].T.astype(out.dtype)


def partial_sums(where, tok, grad_t, weights, units, dtype, after=()):
    total, width = tok.shape
    return pl.pallas_call(
        sums_kernel,
        grid_spec=pltpu.PrefetchScalarGridSpec(
            num_scalar_prefetch=1,
            grid=(width // CHUNK,),
            in_specs=[
                pl.BlockSpec((total, CHUNK), lambda i, w: (0, i)),
                pl.BlockSpec((CHUNK, total), lambda i, w: (i, 0)),
                *weight_specs(units),
                *[HOLD] * len(after),
            ],
            out_specs=pl.BlockSpec((3, total, units), lambda i, w: (0, 0, 0)),
            scratch_shapes=[
                pltpu.VMEM((total, units), F32),
                pltpu.VMEM((total, units), F32),
                pltpu.VMEM((units, total), F32),
            ],
        ),
        out_shape=array((3, total, units), dtype),
        compiler_params=PARAMS,
        cost_estimate=estimate(6 * total * width * units, 6 * width * units),
        name="partial_sums",
    )(where, tok, grad_t, *weights, *after)


def combine_kernel(own, other, out):
    out[...] = (own[...] + other[...].astype(F32)).astype(BF16)


def combine(own, other):
    return pl.pallas_call(
        combine_kernel,
        out_shape=array(own.shape, BF16),
        compiler_params=PARAMS,
        cost_estimate=estimate(own.size, 8 * own.size),
        name="combine",
    )(own, other)


def activate_kernel(own, *refs):
    others, out = refs[:-1], refs[-1]
    gate, up, hidden_grad = (
        functools.reduce(lambda s, o: s + o[j].astype(F32), others, own[j]) for j in range(3)
    )
    sig = jax.nn.sigmoid(gate)
    swish = gate * sig
    out[0] = (swish * up).astype(BF16)
    out[1] = (hidden_grad * up * sig * (1.0 + gate * (1.0 - sig))).astype(BF16)
    out[2] = (hidden_grad * swish).astype(BF16)


def activate(own, others):
    return pl.pallas_call(
        activate_kernel,
        out_shape=array(own.shape, BF16),
        compiler_params=PARAMS,
        cost_estimate=estimate(8 * own.size, 12 * own.size),
        name="activate",
    )(own, *others)


def turned(x):
    return x.astype(F32).T.astype(BF16)


def use_kernel(first, last, with_products, with_grads, where, act, *refs):
    refs = list(refs)
    step = pl.program_id(0)
    if with_products:
        gate_w, up_w, down_w = (refs.pop(0) for _ in range(3))
        before = None if first else refs.pop(0)
    if with_grads:
        tok_t, grad = refs.pop(0), refs.pop(0)
    gate_t, up_t, hidden_t = refs[-3:]
    outs = refs[-3 - (1 + last) * with_products - 3 * with_grads : -3]

    @pl.when(step == 0)
    def _():
        gate_t[...] = turned(act[1])
        up_t[...] = turned(act[2])
        hidden_t[...] = turned(act[0])

    if with_products:
        back = dot(gate_w[...], gate_t[...]) + dot(up_w[...], up_t[...])
        for j, term in enumerate((dot(act[0], down_w[...]), back.T)):
            term = term if first else before[j] + term
            if last:
                half = term.shape[0] // 2
                outs[0][j] = term[:half]
                outs[1][j] = term[half:]
            else:
                outs[0][j] = term
    if with_grads:
        gate_g, up_g, down_g = outs[-3:]
        gate_g[...] = dot(tok_t[...], act[1]).astype(BF16)
        up_g[...] = dot(tok_t[...], act[2]).astype(BF16)
        rows = down_g.shape[0]
        start = pl.multiple_of(step * rows, rows)
        down_g[...] = dot(hidden_t[pl.ds(start, rows)], grad[...]).astype(BF16)


def use(where, act, weights=None, terms=None, last=False, sides=None, grads=(), after=()):
    _, total, units = act.shape
    first = terms is None
    specs = [pl.BlockSpec((3, total, units), lambda i, w: (0, 0, 0))]
    args, out_specs, out_shape, aliases = [act], [], [], {}
    moved = 0
    if weights is not None:
        all_units, width = weights[2].shape
        specs += weight_specs(units)
        args += weights
        if not first:
            specs.append(pl.BlockSpec((2, total, CHUNK), lambda i, w: (0, 0, i)))
            args.append(terms)
        held = total // 2 if last else total
        out_specs += [pl.BlockSpec((2, held, CHUNK), lambda i, w: (0, 0, i))] * (1 + last)
        out_shape += [array((2, held, width), F32)] * (1 + last)
        moved += 6 * width * units
    if sides is not None:
        tok_t, grad, all_units = sides
        width = grad.shape[1]
        steps = width // CHUNK
        rows = units // steps
        specs += [
            pl.BlockSpec((CHUNK, total), lambda i, w: (i, 0)),
            pl.BlockSpec((total, width), lambda i, w: (0, 0)),
        ]
        args += [tok_t, grad]
        for j, grad_before in enumerate(grads):
            aliases[1 + len(args)] = len(out_shape) + j
            specs.append(HOLD)
            args.append(grad_before)
        wide = pl.BlockSpec((CHUNK, units), lambda i, w: (i, w[0]))
        out_specs += [wide, wide, pl.BlockSpec((rows, width), lambda i, w: (w[0] * steps + i, 0))]
        out_shape += [array((width, all_units), BF16)] * 2 + [array((all_units, width), BF16)]
        moved += 6 * width * units
    return pl.pallas_call(
        functools.partial(use_kernel, first, last, weights is not None, sides is not None),
        grid_spec=pltpu.PrefetchScalarGridSpec(
            num_scalar_prefetch=1,
            grid=(width // CHUNK,),
            in_specs=specs + [HOLD] * len(after),
            out_specs=out_specs,
            scratch_shapes=[pltpu.VMEM((units, total), BF16)] * 3,
        ),
        out_shape=out_shape,
        input_output_aliases=aliases,
        compiler_params=PARAMS,
        cost_estimate=estimate(total * moved, moved),
        name=("products" if weights else "") + ("grads" if sides else ""),
    )(where, *args, *after)


def fold_kernel(rows, own, other, keep, *sent):
    total = own[...] + other[...]
    keep[...] = total[:, :rows]
    for i, out in enumerate(sent, 1):
        out[...] = total[:, i * rows : (i + 1) * rows].astype(BF16)


def fold(own, other, rows):
    _, total, width = own.shape
    others = total // rows - 1
    return pl.pallas_call(
        functools.partial(fold_kernel, rows),
        out_shape=[array((2, rows, width), F32)] + [array((2, rows, width), BF16)] * others,
        compiler_params=PARAMS,
        cost_estimate=estimate(own.size, 12 * own.size),
        name="fold",
    )(own, other)


def finish_kernel(own, *refs):
    others, outs = refs[:-2], refs[-2:]
    for j, out in enumerate(outs):
        total = functools.reduce(lambda s, o: s + o[j].astype(F32), others, own[j])
        out[...] = total.astype(BF16)


def finish(own, others):
    return pl.pallas_call(
        finish_kernel,
        out_shape=[array(own.shape[1:], BF16)] * 2,
        compiler_params=PARAMS,
        cost_estimate=estimate(own.size, 12 * own.size),
        name="finish",
    )(own, *others)


def pairwise(n_row, n_col, tokens, gate_weight, up_weight, down_weight, out_grad):
    rows = tokens.shape[0]
    all_units = gate_weight.shape[1]
    units = all_units // n_col
    weights = (gate_weight, up_weight, down_weight)
    col = lax.axis_index("col")
    where = {k: jnp.bitwise_xor(col, k).reshape(1) for k in range(n_col)}
    along_row = functools.partial(swap, axis="row", size=n_row)
    along_col = functools.partial(swap, axis="col", size=n_col)

    mine = pack(tokens, out_grad)
    even = [mine] + [along_row(mine, k=k) for k in range(2, n_row, 2)]
    odd = [along_row(piece, k=1) for piece in even]
    tok, grad, tok_t, grad_t = assemble(even + odd, rows)
    sides = (tok_t, grad, all_units)

    sums = functools.partial(partial_sums, tok=tok, grad_t=grad_t, weights=weights, units=units)
    near = along_col(sums(where[3], dtype=BF16), k=1)
    pair = combine(sums(where[2], dtype=F32), near)
    from_far = along_col(pair, k=2)
    from_near = along_col(sums(where[1], dtype=BF16, after=(pair,)), k=1)
    own = activate(sums(where[0], dtype=F32), [from_near, from_far])

    far_act = along_col(own, k=2)
    near_act = along_col(own, k=1)
    terms, *grads = use(where[0], own, weights, sides=sides)
    held, _ = lax.optimization_barrier((far_act, (terms, grads)))
    last_act = along_col(held, k=1)
    terms, *grads = use(where[1], near_act, weights, terms, sides=sides, grads=grads)
    (terms,) = use(where[2], far_act, weights, terms)
    kept, given = use(where[3], last_act, weights, terms, last=True)

    other = along_row(given, k=1)
    grads = use(where[2], far_act, sides=sides, grads=grads, after=(given,))
    other, _ = lax.optimization_barrier((other, grads))
    mine, *sent = fold(kept, other, rows)
    parts = [along_row(piece, k=2 * i) for i, piece in enumerate(sent, 1)]
    grads = use(where[3], last_act, sides=sides, grads=grads, after=(mine,))
    mixed, input_grad = finish(mine, parts)
    return (mixed, input_grad, *grads)


def gathered(tokens, gate_weight, up_weight, down_weight, out_grad):
    tok = lax.all_gather(tokens, "row", axis=0, tiled=True)
    grad = lax.all_gather(out_grad, "row", axis=0, tiled=True)

    def total(x):
        return lax.psum_scatter(x, "col", scatter_dimension=0, tiled=True)

    def back_dot(a, b):
        return lax.dot_general(a, b, BACK, preferred_element_type=F32)

    def outer(a, b):
        return lax.dot_general(a, b, CONTRACT, preferred_element_type=F32).astype(BF16)

    gate, up = total(dot(tok, gate_weight)), total(dot(tok, up_weight))
    hidden_grad = total(back_dot(grad, down_weight))
    sig = jax.nn.sigmoid(gate)
    swish = gate * sig
    hidden = (swish * up).astype(BF16)
    gate_delta = (hidden_grad * up * sig * (1.0 + gate * (1.0 - sig))).astype(BF16)
    up_delta = (hidden_grad * swish).astype(BF16)
    hidden, gate_delta, up_delta = (
        lax.all_gather(x, "col", axis=0, tiled=True) for x in (hidden, gate_delta, up_delta)
    )
    mixed = dot(hidden, down_weight)
    input_grad = back_dot(gate_delta, gate_weight) + back_dot(up_delta, up_weight)
    mixed, input_grad = (
        lax.psum_scatter(x, "row", scatter_dimension=0, tiled=True).astype(BF16)
        for x in (mixed, input_grad)
    )
    return (
        mixed,
        input_grad,
        outer(tok, gate_delta),
        outer(tok, up_delta),
        outer(hidden, grad),
    )


def solution(mesh):
    n_row, n_col = mesh.shape["row"], mesh.shape["col"]

    def shards(*args):
        tokens, gate_weight = args[:2]
        fits = (
            n_row & (n_row - 1) == 0
            and n_row > 1
            and n_col == 4
            and tokens.shape[0] % 8 == 0
            and tokens.shape[1] % CHUNK == 0
            and gate_weight.shape[1] % (128 * n_col) == 0
            and gate_weight.shape[1] % (16 * n_col * (tokens.shape[1] // CHUNK)) == 0
        )
        if fits:
            return pairwise(n_row, n_col, *args)
        return gathered(*args)

    return jax.shard_map(
        shards,
        mesh=mesh,
        in_specs=(
            P("row", "col"),
            P("col", "row"),
            P("col", "row"),
            P("row", "col"),
            P("row", "col"),
        ),
        out_specs=(
            P("row", "col"),
            P("row", "col"),
            P("col", "row"),
            P("col", "row"),
            P("row", "col"),
        ),
        check_vma=False,
    )
```

```python
import functools

import jax
import jax.numpy as jnp
from jax import lax
from jax.experimental import pallas as pl
from jax.experimental.pallas import tpu as pltpu
from jax.sharding import PartitionSpec as P

BF16 = jnp.bfloat16
F32 = jnp.float32
VMEM_LIMIT = 48 * 1024 * 1024
CHUNKS = 4
BACK = (((1,), (1,)), ((), ()))
CONTRACT = (((0,), (0,)), ((), ()))
PARAMS = pltpu.CompilerParams(vmem_limit_bytes=VMEM_LIMIT)
HOLD = pl.BlockSpec(memory_space=pl.ANY)
WHOLE = pl.BlockSpec(memory_space=pltpu.VMEM)


def dot(a, b):
    return jnp.dot(a, b, preferred_element_type=F32)


def swap(x, axis, size, k):
    return lax.ppermute(x, axis, [(i, i ^ k) for i in range(size)])


def estimate(flops, num_bytes):
    return pl.CostEstimate(flops=flops // 8, bytes_accessed=num_bytes // 8, transcendentals=0)


def in_hbm(arrays):
    return [pltpu.with_memory_space_constraint(x, pltpu.HBM) for x in arrays]


def array(shape, dtype):
    return jax.ShapeDtypeStruct(shape, dtype)


def pack_kernel(tokens, out_grad, out):
    joined = jnp.concatenate([tokens[...].astype(F32), out_grad[...].astype(F32)], axis=0)
    out[...] = joined.astype(BF16)


def pack(tokens, out_grad):
    rows, width = tokens.shape
    return pl.pallas_call(
        pack_kernel,
        out_shape=array((2 * rows, width), BF16),
        compiler_params=PARAMS,
        cost_estimate=estimate(0, 8 * rows * width),
        name="pack",
    )(*in_hbm((tokens, out_grad)))


def assemble_kernel(rows, *refs):
    pieces, (tok, grad, tok_t, grad_t) = refs[:-4], refs[-4:]
    both = [p[...].astype(F32) for p in pieces]
    all_tok = jnp.concatenate([b[:rows] for b in both], axis=0)
    all_grad = jnp.concatenate([b[rows:] for b in both], axis=0)
    tok[...] = all_tok.astype(BF16)
    grad[...] = all_grad.astype(BF16)
    tok_t[...] = all_tok.T.astype(BF16)
    grad_t[...] = all_grad.T.astype(BF16)


def assemble(pieces, rows):
    total, width = rows * len(pieces), pieces[0].shape[1]
    flat, turned = (total, width), (width, total)
    return pl.pallas_call(
        functools.partial(assemble_kernel, rows),
        out_shape=[array(shape, BF16) for shape in (flat, flat, turned, turned)],
        compiler_params=PARAMS,
        cost_estimate=estimate(0, 12 * total * width),
        name="assemble",
    )(*pieces)


def unit_block(k, units):
    start = jnp.bitwise_xor(lax.axis_index("col"), k) * units
    return pl.ds(pl.multiple_of(start, units), units)


def span(i, size):
    return slice(i * size, (i + 1) * size)


def fetches(k, hbm, vmem, sems):
    units, width = vmem[2].shape
    mine = unit_block(k, units)
    part = width // CHUNKS
    copies = []
    for i in range(CHUNKS):
        rows = pl.ds(i * part, part)
        ends = [
            (hbm[0].at[rows, mine], vmem[0].at[rows]),
            (hbm[1].at[rows, mine], vmem[1].at[rows]),
            (hbm[2].at[mine, rows], vmem[2].at[:, rows]),
        ]
        copies.append(
            [pltpu.make_async_copy(*ends[j], sems.at[i, j]) for j in range(len(ends))]
        )
    return copies


def weight_scratch(units, width):
    return [
        pltpu.VMEM((width, units), BF16),
        pltpu.VMEM((width, units), BF16),
        pltpu.VMEM((units, width), BF16),
        pltpu.SemaphoreType.DMA((CHUNKS, 3)),
    ]


def sums_kernel(k, tok, grad_t, gate_w, up_w, down_w, *refs):
    out, gate_b, up_b, down_b, sems, gate, up, back = refs[-8:]
    copies = fetches(k, (gate_w, up_w, down_w), (gate_b, up_b, down_b), sems)
    for chunk in copies:
        for copy in chunk:
            copy.start()
    part = grad_t.shape[0] // CHUNKS
    for i, chunk in enumerate(copies):
        here = span(i, part)
        for copy in chunk:
            copy.wait()
        terms = (
            (gate, dot(tok[:, here], gate_b[here])),
            (up, dot(tok[:, here], up_b[here])),
            (back, dot(down_b[:, here], grad_t[here])),
        )
        for acc, term in terms:
            if i == 0:
                acc[...] = term
            else:
                acc[...] += term
    out[0] = gate[...].astype(out.dtype)
    out[1] = up[...].astype(out.dtype)
    out[2] = back[...].T.astype(out.dtype)


def partial_sums(k, tok, grad_t, weights, units, dtype, after=()):
    total, width = tok.shape
    return pl.pallas_call(
        functools.partial(sums_kernel, k),
        in_specs=[WHOLE, WHOLE] + [HOLD] * (3 + len(after)),
        out_specs=WHOLE,
        scratch_shapes=weight_scratch(units, width)
        + [
            pltpu.VMEM((total, units), F32),
            pltpu.VMEM((total, units), F32),
            pltpu.VMEM((units, total), F32),
        ],
        out_shape=array((3, total, units), dtype),
        compiler_params=PARAMS,
        cost_estimate=estimate(6 * total * width * units, 6 * width * units),
        name="partial_sums",
    )(tok, grad_t, *in_hbm(weights), *after)


def combine_kernel(own, other, out):
    out[...] = (own[...] + other[...].astype(F32)).astype(BF16)


def combine(own, other):
    return pl.pallas_call(
        combine_kernel,
        out_shape=array(own.shape, BF16),
        compiler_params=PARAMS,
        cost_estimate=estimate(own.size, 8 * own.size),
        name="combine",
    )(own, other)


def activate_kernel(own, *refs):
    others, out = refs[:-1], refs[-1]
    gate, up, hidden_grad = (
        functools.reduce(lambda s, o: s + o[j].astype(F32), others, own[j]) for j in range(3)
    )
    sig = jax.nn.sigmoid(gate)
    swish = gate * sig
    out[0] = (swish * up).astype(BF16)
    out[1] = (hidden_grad * up * sig * (1.0 + gate * (1.0 - sig))).astype(BF16)
    out[2] = (hidden_grad * swish).astype(BF16)


def activate(own, others):
    return pl.pallas_call(
        activate_kernel,
        out_shape=array(own.shape, BF16),
        compiler_params=PARAMS,
        cost_estimate=estimate(8 * own.size, 12 * own.size),
        name="activate",
    )(own, *others)


def turned(x):
    return x.astype(F32).T.astype(BF16)


def use_kernel(k, first, last, with_products, with_grads, act, *refs):
    refs = list(refs)
    width = 0
    if with_products:
        weights = [refs.pop(0) for _ in range(3)]
        before = None if first else refs.pop(0)
        width = weights[2].shape[1]
    if with_grads:
        tok_t, grad = refs.pop(0), refs.pop(0)
        width = grad.shape[1]
    units = act.shape[2]
    if with_grads:
        gate_s, up_s, down_s, out_sems = refs[-4:]
        refs = refs[:-4]
    if with_products:
        gate_b, up_b, down_b, sems = refs[-4:]
        refs = refs[:-4]
    outs = refs[-(1 + last) * with_products - 3 * with_grads :]
    part, rows = width // CHUNKS, units // CHUNKS

    arriving, leaving = [], []
    if with_products:
        arriving = fetches(k, weights, (gate_b, up_b, down_b), sems)
        for chunk in arriving:
            for copy in chunk:
                copy.start()
        gate_t, up_t = turned(act[1]), turned(act[2])
    if with_grads:
        hidden_t = turned(act[0])
        mine = unit_block(k, units)
        start = jnp.bitwise_xor(lax.axis_index("col"), k) * units
    for i in range(CHUNKS):
        here = span(i, part)
        if with_grads:
            gate_g, up_g, down_g = outs[-3:]
            gate_s[here] = dot(tok_t[here], act[1]).astype(BF16)
            up_s[here] = dot(tok_t[here], act[2]).astype(BF16)
            some = span(i, rows)
            down_s[some] = dot(hidden_t[some], grad[...]).astype(BF16)
            there = pl.ds(i * part, part)
            below = pl.ds(pl.multiple_of(start + i * rows, rows), rows)
            ends = (
                (gate_s.at[there], gate_g.at[there, mine]),
                (up_s.at[there], up_g.at[there, mine]),
                (down_s.at[pl.ds(i * rows, rows)], down_g.at[below]),
            )
            for j, (source, target) in enumerate(ends):
                copy = pltpu.make_async_copy(source, target, out_sems.at[i, j])
                copy.start()
                leaving.append(copy)
        if with_products:
            for copy in arriving[i]:
                copy.wait()
            back = dot(gate_b[here], gate_t) + dot(up_b[here], up_t)
            for j, term in enumerate((dot(act[0], down_b[:, here]), back.T)):
                term = term if first else before[j, :, here] + term
                if last:
                    half = term.shape[0] // 2
                    outs[0][j, :, here] = term[:half]
                    outs[1][j, :, here] = term[half:]
                else:
                    outs[0][j, :, here] = term
    for copy in leaving:
        copy.wait()


def use(k, act, weights=None, terms=None, last=False, sides=None, grads=(), after=()):
    _, total, units = act.shape
    first = terms is None
    specs, args = [WHOLE], [act]
    out_specs, out_shape, scratch, aliases = [], [], [], {}
    moved = 0
    if weights is not None:
        width = weights[2].shape[1]
        specs += [HOLD] * 3
        args += in_hbm(weights)
        if not first:
            specs.append(WHOLE)
            args.append(terms)
        held = total // 2 if last else total
        out_specs += [WHOLE] * (1 + last)
        out_shape += [array((2, held, width), F32)] * (1 + last)
        scratch += weight_scratch(units, width)
        moved += 6 * width * units
    if sides is not None:
        tok_t, grad, all_units = sides
        width = grad.shape[1]
        specs += [WHOLE, WHOLE]
        args += [tok_t, grad]
        for j, grad_before in enumerate(grads):
            aliases[len(args)] = len(out_shape) + j
            specs.append(HOLD)
            args.append(grad_before)
        out_specs += [HOLD] * 3
        out_shape += [pltpu.HBM((width, all_units), BF16)] * 2
        out_shape.append(pltpu.HBM((all_units, width), BF16))
        scratch += weight_scratch(units, width)
        moved += 6 * width * units
    return pl.pallas_call(
        functools.partial(use_kernel, k, first, last, weights is not None, sides is not None),
        in_specs=specs + [HOLD] * len(after),
        out_specs=out_specs,
        scratch_shapes=scratch,
        out_shape=out_shape,
        input_output_aliases=aliases,
        compiler_params=PARAMS,
        cost_estimate=estimate(total * moved, moved),
        name=("products" if weights else "") + ("grads" if sides else ""),
    )(*args, *after)


def fold_kernel(rows, own, other, keep, *sent):
    total = own[...] + other[...]
    keep[...] = total[:, :rows]
    for i, out in enumerate(sent, 1):
        out[...] = total[:, i * rows : (i + 1) * rows].astype(BF16)


def fold(own, other, rows):
    _, total, width = own.shape
    others = total // rows - 1
    return pl.pallas_call(
        functools.partial(fold_kernel, rows),
        out_shape=[array((2, rows, width), F32)] + [array((2, rows, width), BF16)] * others,
        compiler_params=PARAMS,
        cost_estimate=estimate(own.size, 12 * own.size),
        name="fold",
    )(own, other)


def finish_kernel(own, *refs):
    others, outs = refs[:-2], refs[-2:]
    for j, out in enumerate(outs):
        total = functools.reduce(lambda s, o: s + o[j].astype(F32), others, own[j])
        out[...] = total.astype(BF16)


def finish(own, others):
    return pl.pallas_call(
        finish_kernel,
        out_shape=[array(own.shape[1:], BF16)] * 2,
        compiler_params=PARAMS,
        cost_estimate=estimate(own.size, 12 * own.size),
        name="finish",
    )(own, *others)


def pairwise(n_row, n_col, tokens, gate_weight, up_weight, down_weight, out_grad):
    rows = tokens.shape[0]
    all_units = gate_weight.shape[1]
    units = all_units // n_col
    weights = (gate_weight, up_weight, down_weight)
    along_row = functools.partial(swap, axis="row", size=n_row)
    along_col = functools.partial(swap, axis="col", size=n_col)

    mine = pack(tokens, out_grad)
    even = [mine] + [along_row(mine, k=k) for k in range(2, n_row, 2)]
    odd = [along_row(piece, k=1) for piece in even]
    tok, grad, tok_t, grad_t = assemble(even + odd, rows)
    sides = (tok_t, grad, all_units)

    sums = functools.partial(partial_sums, tok=tok, grad_t=grad_t, weights=weights, units=units)
    near = along_col(sums(3, dtype=BF16), k=1)
    pair = combine(sums(2, dtype=F32), near)
    from_far = along_col(pair, k=2)
    from_near = along_col(sums(1, dtype=BF16), k=1)
    own = activate(sums(0, dtype=F32), [from_near, from_far])

    far_act = along_col(own, k=2)
    near_act = along_col(own, k=1)
    terms, *grads = use(0, own, weights, sides=sides)
    held, _ = lax.optimization_barrier((far_act, (terms, grads)))
    last_act = along_col(held, k=1)
    terms, *grads = use(1, near_act, weights, terms, sides=sides, grads=grads)
    (terms,) = use(2, far_act, weights, terms)
    kept, given = use(3, last_act, weights, terms, last=True)

    other = along_row(given, k=1)
    grads = use(2, far_act, sides=sides, grads=grads, after=(given,))
    other, _ = lax.optimization_barrier((other, grads))
    mine, *sent = fold(kept, other, rows)
    parts = [along_row(piece, k=2 * i) for i, piece in enumerate(sent, 1)]
    grads = use(3, last_act, sides=sides, grads=grads, after=(mine,))
    mixed, input_grad = finish(mine, parts)
    return (mixed, input_grad, *grads)


def gathered(tokens, gate_weight, up_weight, down_weight, out_grad):
    tok = lax.all_gather(tokens, "row", axis=0, tiled=True)
    grad = lax.all_gather(out_grad, "row", axis=0, tiled=True)

    def total(x):
        return lax.psum_scatter(x, "col", scatter_dimension=0, tiled=True)

    def back_dot(a, b):
        return lax.dot_general(a, b, BACK, preferred_element_type=F32)

    def outer(a, b):
        return lax.dot_general(a, b, CONTRACT, preferred_element_type=F32).astype(BF16)

    gate, up = total(dot(tok, gate_weight)), total(dot(tok, up_weight))
    hidden_grad = total(back_dot(grad, down_weight))
    sig = jax.nn.sigmoid(gate)
    swish = gate * sig
    hidden = (swish * up).astype(BF16)
    gate_delta = (hidden_grad * up * sig * (1.0 + gate * (1.0 - sig))).astype(BF16)
    up_delta = (hidden_grad * swish).astype(BF16)
    hidden, gate_delta, up_delta = (
        lax.all_gather(x, "col", axis=0, tiled=True) for x in (hidden, gate_delta, up_delta)
    )
    mixed = dot(hidden, down_weight)
    input_grad = back_dot(gate_delta, gate_weight) + back_dot(up_delta, up_weight)
    mixed, input_grad = (
        lax.psum_scatter(x, "row", scatter_dimension=0, tiled=True).astype(BF16)
        for x in (mixed, input_grad)
    )
    return (
        mixed,
        input_grad,
        outer(tok, gate_delta),
        outer(tok, up_delta),
        outer(hidden, grad),
    )


def solution(mesh):
    n_row, n_col = mesh.shape["row"], mesh.shape["col"]

    def shards(*args):
        tokens, gate_weight = args[:2]
        fits = (
            n_row & (n_row - 1) == 0
            and n_row > 1
            and n_col == 4
            and tokens.shape[0] % 8 == 0
            and tokens.shape[1] % (128 * CHUNKS) == 0
            and gate_weight.shape[1] % (128 * n_col) == 0
            and gate_weight.shape[1] % (16 * CHUNKS * n_col) == 0
            and 3 * gate_weight.size <= 24 * 1024 * 1024
        )
        if fits:
            return pairwise(n_row, n_col, *args)
        return gathered(*args)

    return jax.shard_map(
        shards,
        mesh=mesh,
        in_specs=(
            P("row", "col"),
            P("col", "row"),
            P("col", "row"),
            P("row", "col"),
            P("row", "col"),
        ),
        out_specs=(
            P("row", "col"),
            P("row", "col"),
            P("col", "row"),
            P("col", "row"),
            P("row", "col"),
        ),
        check_vma=False,
    )
```

```python
import functools

import jax
import jax.numpy as jnp
from jax import lax
from jax.experimental import pallas as pl
from jax.experimental.pallas import tpu as pltpu
from jax.sharding import PartitionSpec as P

BF16 = jnp.bfloat16
F32 = jnp.float32
VMEM_LIMIT = 48 * 1024 * 1024
CHUNKS = 8
BACK = (((1,), (1,)), ((), ()))
CONTRACT = (((0,), (0,)), ((), ()))
PARAMS = pltpu.CompilerParams(vmem_limit_bytes=VMEM_LIMIT)
HOLD = pl.BlockSpec(memory_space=pl.ANY)
WHOLE = pl.BlockSpec(memory_space=pltpu.VMEM)


def dot(a, b):
    return jnp.dot(a, b, preferred_element_type=F32)


def back_dot(a, b):
    return lax.dot_general(a, b, BACK, preferred_element_type=F32)


def swap(x, axis, size, k):
    return lax.ppermute(x, axis, [(i, i ^ k) for i in range(size)])


def estimate(flops, num_bytes):
    return pl.CostEstimate(flops=flops // 8, bytes_accessed=num_bytes // 8, transcendentals=0)


def in_hbm(arrays):
    return [pltpu.with_memory_space_constraint(x, pltpu.HBM) for x in arrays]


def array(shape, dtype):
    return jax.ShapeDtypeStruct(shape, dtype)


def pack_kernel(tokens, out_grad, out):
    joined = jnp.concatenate([tokens[...].astype(F32), out_grad[...].astype(F32)], axis=0)
    out[...] = joined.astype(BF16)


def pack(tokens, out_grad):
    rows, width = tokens.shape
    return pl.pallas_call(
        pack_kernel,
        out_shape=array((2 * rows, width), BF16),
        compiler_params=PARAMS,
        cost_estimate=estimate(0, 8 * rows * width),
        name="pack",
    )(*in_hbm((tokens, out_grad)))


def assemble_kernel(rows, *refs):
    pieces, (tok, grad, tok_t) = refs[:-3], refs[-3:]
    both = [p[...].astype(F32) for p in pieces]
    all_tok = jnp.concatenate([b[:rows] for b in both], axis=0)
    all_grad = jnp.concatenate([b[rows:] for b in both], axis=0)
    tok[...] = all_tok.astype(BF16)
    grad[...] = all_grad.astype(BF16)
    tok_t[...] = all_tok.T.astype(BF16)


def assemble(pieces, rows):
    total, width = rows * len(pieces), pieces[0].shape[1]
    flat = (total, width)
    return pl.pallas_call(
        functools.partial(assemble_kernel, rows),
        out_shape=[array(shape, BF16) for shape in (flat, flat, (width, total))],
        compiler_params=PARAMS,
        cost_estimate=estimate(0, 12 * total * width),
        name="assemble",
    )(*pieces)


def unit_block(k, units):
    start = jnp.bitwise_xor(lax.axis_index("col"), k) * units
    return pl.ds(pl.multiple_of(start, units), units)


def span(i, size):
    return slice(i * size, (i + 1) * size)


def fetches(k, hbm, vmem, sems):
    units, width = vmem[2].shape
    mine = unit_block(k, units)
    part = width // CHUNKS
    copies = []
    for i in range(CHUNKS):
        rows = pl.ds(i * part, part)
        ends = [
            (hbm[0].at[rows, mine], vmem[0].at[rows]),
            (hbm[1].at[rows, mine], vmem[1].at[rows]),
            (hbm[2].at[mine, rows], vmem[2].at[:, rows]),
        ]
        copies.append(
            [pltpu.make_async_copy(*ends[j], sems.at[i, j]) for j in range(len(ends))]
        )
    return copies


def weight_scratch(units, width):
    return [
        pltpu.VMEM((width, units), BF16),
        pltpu.VMEM((width, units), BF16),
        pltpu.VMEM((units, width), BF16),
        pltpu.SemaphoreType.DMA((CHUNKS, 3)),
    ]


def sums_kernel(k, tok, grad, gate_w, up_w, down_w, *refs):
    out, gate_b, up_b, down_b, sems, gate, up, back = refs[-8:]
    copies = fetches(k, (gate_w, up_w, down_w), (gate_b, up_b, down_b), sems)
    for chunk in copies:
        for copy in chunk:
            copy.start()
    part = grad.shape[1] // CHUNKS
    for i, chunk in enumerate(copies):
        here = span(i, part)
        for copy in chunk:
            copy.wait()
        terms = (
            (gate, dot(tok[:, here], gate_b[here])),
            (up, dot(tok[:, here], up_b[here])),
            (back, back_dot(grad[:, here], down_b[:, here])),
        )
        for acc, term in terms:
            if i == 0:
                acc[...] = term
            else:
                acc[...] += term
    out[0] = gate[...].astype(out.dtype)
    out[1] = up[...].astype(out.dtype)
    out[2] = back[...].astype(out.dtype)


def partial_sums(k, tok, grad, weights, units, dtype, after=()):
    total, width = tok.shape
    return pl.pallas_call(
        functools.partial(sums_kernel, k),
        in_specs=[WHOLE, WHOLE] + [HOLD] * (3 + len(after)),
        out_specs=WHOLE,
        scratch_shapes=weight_scratch(units, width)
        + [pltpu.VMEM((total, units), F32)] * 3,
        out_shape=array((3, total, units), dtype),
        compiler_params=PARAMS,
        cost_estimate=estimate(6 * total * width * units, 6 * width * units),
        name="partial_sums",
    )(tok, grad, *in_hbm(weights), *after)


def combine_kernel(own, other, out):
    out[...] = (own[...] + other[...].astype(F32)).astype(BF16)


def combine(own, other):
    return pl.pallas_call(
        combine_kernel,
        out_shape=array(own.shape, BF16),
        compiler_params=PARAMS,
        cost_estimate=estimate(own.size, 8 * own.size),
        name="combine",
    )(own, other)


def activate_kernel(own, *refs):
    others, out = refs[:-1], refs[-1]
    gate, up, hidden_grad = (
        functools.reduce(lambda s, o: s + o[j].astype(F32), others, own[j]) for j in range(3)
    )
    sig = jax.nn.sigmoid(gate)
    swish = gate * sig
    out[0] = (swish * up).astype(BF16)
    out[1] = (hidden_grad * up * sig * (1.0 + gate * (1.0 - sig))).astype(BF16)
    out[2] = (hidden_grad * swish).astype(BF16)


def activate(own, others):
    return pl.pallas_call(
        activate_kernel,
        out_shape=array(own.shape, BF16),
        compiler_params=PARAMS,
        cost_estimate=estimate(8 * own.size, 12 * own.size),
        name="activate",
    )(own, *others)


def use_kernel(k, chunks, first, last, with_products, with_grads, act, *refs):
    refs = list(refs)
    width = 0
    if with_products:
        weights = [refs.pop(0) for _ in range(3)]
        before = None if first else refs.pop(0)
        width = weights[2].shape[1]
    if with_grads:
        tok_t, grad = refs.pop(0), refs.pop(0)
        width = grad.shape[1]
    units = act.shape[2]
    if with_grads:
        gate_s, up_s, down_s, out_sems = refs[-4:]
        refs = refs[:-4]
    if with_products:
        gate_b, up_b, down_b, sems = refs[-4:]
        refs = refs[:-4]
    outs = refs[-(1 + last) * with_products - 3 * with_grads :]
    part, rows = width // CHUNKS, units // CHUNKS

    arriving, leaving = [], []
    if with_products:
        arriving = fetches(k, weights, (gate_b, up_b, down_b), sems)
        for chunk in arriving:
            for copy in chunk:
                copy.start()
    if with_grads:
        hidden_t = act[0].astype(F32).T.astype(BF16)
        mine = unit_block(k, units)
        start = jnp.bitwise_xor(lax.axis_index("col"), k) * units
    for i in chunks:
        here = span(i, part)
        if with_grads:
            gate_g, up_g, down_g = outs[-3:]
            gate_s[here] = dot(tok_t[here], act[1]).astype(BF16)
            up_s[here] = dot(tok_t[here], act[2]).astype(BF16)
            some = span(i, rows)
            down_s[some] = dot(hidden_t[some], grad[...]).astype(BF16)
            there = pl.ds(i * part, part)
            below = pl.ds(pl.multiple_of(start + i * rows, rows), rows)
            ends = (
                (gate_s.at[there], gate_g.at[there, mine]),
                (up_s.at[there], up_g.at[there, mine]),
                (down_s.at[pl.ds(i * rows, rows)], down_g.at[below]),
            )
            for j, (source, target) in enumerate(ends):
                copy = pltpu.make_async_copy(source, target, out_sems.at[i, j])
                copy.start()
                leaving.append(copy)
        if with_products:
            for copy in arriving[i]:
                copy.wait()
            back = back_dot(act[1], gate_b[here]) + back_dot(act[2], up_b[here])
            for j, term in enumerate((dot(act[0], down_b[:, here]), back)):
                term = term if first else before[j, :, here] + term
                if last:
                    half = term.shape[0] // 2
                    outs[0][j, :, here] = term[:half]
                    outs[1][j, :, here] = term[half:]
                else:
                    outs[0][j, :, here] = term
    for copy in leaving:
        copy.wait()


def use(
    k,
    act,
    weights=None,
    terms=None,
    last=False,
    sides=None,
    grads=(),
    after=(),
    chunks=range(CHUNKS),
):
    _, total, units = act.shape
    first = terms is None
    specs, args = [WHOLE], [act]
    out_specs, out_shape, scratch, aliases = [], [], [], {}
    moved = 0
    if weights is not None:
        width = weights[2].shape[1]
        specs += [HOLD] * 3
        args += in_hbm(weights)
        if not first:
            specs.append(WHOLE)
            args.append(terms)
        held = total // 2 if last else total
        out_specs += [WHOLE] * (1 + last)
        out_shape += [array((2, held, width), F32)] * (1 + last)
        scratch += weight_scratch(units, width)
        moved += 6 * width * units
    if sides is not None:
        tok_t, grad, all_units = sides
        width = grad.shape[1]
        specs += [WHOLE, WHOLE]
        args += [tok_t, grad]
        for j, grad_before in enumerate(grads):
            aliases[len(args)] = len(out_shape) + j
            specs.append(HOLD)
            args.append(grad_before)
        out_specs += [HOLD] * 3
        out_shape += [pltpu.HBM((width, all_units), BF16)] * 2
        out_shape.append(pltpu.HBM((all_units, width), BF16))
        scratch += weight_scratch(units, width)
        moved += 6 * width * units
    return pl.pallas_call(
        functools.partial(
            use_kernel, k, chunks, first, last, weights is not None, sides is not None
        ),
        in_specs=specs + [HOLD] * len(after),
        out_specs=out_specs,
        scratch_shapes=scratch,
        out_shape=out_shape,
        input_output_aliases=aliases,
        compiler_params=PARAMS,
        cost_estimate=estimate(total * moved, moved),
        name=("products" if weights else "") + ("grads" if sides else ""),
    )(*args, *after)


def fold_kernel(rows, own, other, keep, *sent):
    total = own[...] + other[...]
    keep[...] = total[:, :rows]
    for i, out in enumerate(sent, 1):
        out[...] = total[:, i * rows : (i + 1) * rows].astype(BF16)


def fold(own, other, rows):
    _, total, width = own.shape
    others = total // rows - 1
    return pl.pallas_call(
        functools.partial(fold_kernel, rows),
        out_shape=[array((2, rows, width), F32)] + [array((2, rows, width), BF16)] * others,
        compiler_params=PARAMS,
        cost_estimate=estimate(own.size, 12 * own.size),
        name="fold",
    )(own, other)


def finish_kernel(own, *refs):
    others, outs = refs[:-2], refs[-2:]
    for j, out in enumerate(outs):
        total = functools.reduce(lambda s, o: s + o[j].astype(F32), others, own[j])
        out[...] = total.astype(BF16)


def finish(own, others):
    return pl.pallas_call(
        finish_kernel,
        out_shape=[array(own.shape[1:], BF16)] * 2,
        compiler_params=PARAMS,
        cost_estimate=estimate(own.size, 12 * own.size),
        name="finish",
    )(own, *others)


def pairwise(n_row, n_col, tokens, gate_weight, up_weight, down_weight, out_grad):
    rows = tokens.shape[0]
    all_units = gate_weight.shape[1]
    units = all_units // n_col
    weights = (gate_weight, up_weight, down_weight)
    along_row = functools.partial(swap, axis="row", size=n_row)
    along_col = functools.partial(swap, axis="col", size=n_col)

    mine = pack(tokens, out_grad)
    even = [mine] + [along_row(mine, k=k) for k in range(2, n_row, 2)]
    odd = [along_row(piece, k=1) for piece in even]
    tok, grad, tok_t = assemble(even + odd, rows)
    sides = (tok_t, grad, all_units)

    sums = functools.partial(partial_sums, tok=tok, grad=grad, weights=weights, units=units)
    near = along_col(sums(3, dtype=BF16), k=1)
    pair = combine(sums(2, dtype=F32), near)
    from_far = along_col(pair, k=2)
    from_near = along_col(sums(1, dtype=BF16), k=1)
    own = activate(sums(0, dtype=F32), [from_near, from_far])

    near_act = along_col(own, k=1)
    far_act = along_col(own, k=2)
    terms, *grads = use(0, own, weights, sides=sides)
    terms, *grads = use(1, near_act, weights, terms, sides=sides, grads=grads)
    held, _ = lax.optimization_barrier((far_act, (terms, grads)))
    last_act = along_col(held, k=1)
    terms, *grads = use(2, far_act, weights, terms, sides=sides, grads=grads)
    kept, given = use(3, last_act, weights, terms, last=True)

    other = along_row(given, k=1)
    halves = range(CHUNKS // 2), range(CHUNKS // 2, CHUNKS)
    grads = use(3, last_act, sides=sides, grads=grads, after=(given,), chunks=halves[0])
    other, _ = lax.optimization_barrier((other, grads))
    mine, *sent = fold(kept, other, rows)
    parts = [along_row(piece, k=2 * i) for i, piece in enumerate(sent, 1)]
    grads = use(3, last_act, sides=sides, grads=grads, after=(mine,), chunks=halves[1])
    mixed, input_grad = finish(mine, parts)
    return (mixed, input_grad, *grads)


def gathered(tokens, gate_weight, up_weight, down_weight, out_grad):
    tok = lax.all_gather(tokens, "row", axis=0, tiled=True)
    grad = lax.all_gather(out_grad, "row", axis=0, tiled=True)

    def total(x):
        return lax.psum_scatter(x, "col", scatter_dimension=0, tiled=True)

    def outer(a, b):
        return lax.dot_general(a, b, CONTRACT, preferred_element_type=F32).astype(BF16)

    gate, up = total(dot(tok, gate_weight)), total(dot(tok, up_weight))
    hidden_grad = total(back_dot(grad, down_weight))
    sig = jax.nn.sigmoid(gate)
    swish = gate * sig
    hidden = (swish * up).astype(BF16)
    gate_delta = (hidden_grad * up * sig * (1.0 + gate * (1.0 - sig))).astype(BF16)
    up_delta = (hidden_grad * swish).astype(BF16)
    hidden, gate_delta, up_delta = (
        lax.all_gather(x, "col", axis=0, tiled=True) for x in (hidden, gate_delta, up_delta)
    )
    mixed = dot(hidden, down_weight)
    input_grad = back_dot(gate_delta, gate_weight) + back_dot(up_delta, up_weight)
    mixed, input_grad = (
        lax.psum_scatter(x, "row", scatter_dimension=0, tiled=True).astype(BF16)
        for x in (mixed, input_grad)
    )
    return (
        mixed,
        input_grad,
        outer(tok, gate_delta),
        outer(tok, up_delta),
        outer(hidden, grad),
    )


def solution(mesh):
    n_row, n_col = mesh.shape["row"], mesh.shape["col"]

    def shards(*args):
        tokens, gate_weight = args[:2]
        fits = (
            n_row & (n_row - 1) == 0
            and n_row > 1
            and n_col == 4
            and tokens.shape[0] % 8 == 0
            and tokens.shape[1] % (128 * CHUNKS) == 0
            and gate_weight.shape[1] % (128 * n_col) == 0
            and gate_weight.shape[1] % (16 * CHUNKS * n_col) == 0
            and 3 * gate_weight.size <= 24 * 1024 * 1024
        )
        if fits:
            return pairwise(n_row, n_col, *args)
        return gathered(*args)

    return jax.shard_map(
        shards,
        mesh=mesh,
        in_specs=(
            P("row", "col"),
            P("col", "row"),
            P("col", "row"),
            P("row", "col"),
            P("row", "col"),
        ),
        out_specs=(
            P("row", "col"),
            P("row", "col"),
            P("col", "row"),
            P("col", "row"),
            P("row", "col"),
        ),
        check_vma=False,
    )
```

```python
import functools

import jax
import jax.numpy as jnp
from jax import lax
from jax.experimental import pallas as pl
from jax.experimental.pallas import tpu as pltpu
from jax.sharding import PartitionSpec as P

BF16 = jnp.bfloat16
F32 = jnp.float32
VMEM_LIMIT = 14 * 1024 * 1024
CHUNKS = 8
BACK = (((1,), (1,)), ((), ()))
CONTRACT = (((0,), (0,)), ((), ()))
PARAMS = pltpu.CompilerParams(vmem_limit_bytes=VMEM_LIMIT)
HOLD = pl.BlockSpec(memory_space=pl.ANY)
PIECE = 512
WHOLE = pl.BlockSpec(memory_space=pltpu.VMEM)


def dot(a, b):
    return jnp.dot(a, b, preferred_element_type=F32)


def back_dot(a, b):
    return lax.dot_general(a, b, BACK, preferred_element_type=F32)


def swap(x, axis, size, k):
    return lax.ppermute(x, axis, [(i, i ^ k) for i in range(size)])


def estimate(flops, num_bytes):
    return pl.CostEstimate(flops=flops // 8, bytes_accessed=num_bytes // 8, transcendentals=0)


def vmem_array(shape):
    return pltpu.VMEM(shape, BF16)


def in_vmem(arrays):
    return [pltpu.with_memory_space_constraint(x, pltpu.VMEM) for x in arrays]


def in_hbm(arrays):
    return [pltpu.with_memory_space_constraint(x, pltpu.HBM) for x in arrays]


def array(shape, dtype):
    return jax.ShapeDtypeStruct(shape, dtype)


def pack_kernel(tokens, out_grad, out):
    joined = jnp.concatenate([tokens[...].astype(F32), out_grad[...].astype(F32)], axis=0)
    out[...] = joined.astype(BF16)


def pack(tokens, out_grad):
    rows, width = tokens.shape
    return pl.pallas_call(
        pack_kernel,
        out_shape=array((2 * rows, width), BF16),
        compiler_params=PARAMS,
        cost_estimate=estimate(0, 8 * rows * width),
        name="pack",
    )(*in_hbm((tokens, out_grad)))


def assemble_kernel(rows, *refs):
    pieces, (tok, grad, tok_t) = refs[:-3], refs[-3:]
    both = [p[...].astype(F32) for p in pieces]
    all_tok = jnp.concatenate([b[:rows] for b in both], axis=0)
    all_grad = jnp.concatenate([b[rows:] for b in both], axis=0)
    tok[...] = all_tok.astype(BF16)
    grad[...] = all_grad.astype(BF16)
    tok_t[...] = all_tok.T.astype(BF16)


def assemble(pieces, rows):
    total, width = rows * len(pieces), pieces[0].shape[1]
    flat = (total, width)
    return pl.pallas_call(
        functools.partial(assemble_kernel, rows),
        out_shape=[array(shape, BF16) for shape in (flat, flat, (width, total))],
        compiler_params=PARAMS,
        cost_estimate=estimate(0, 12 * total * width),
        name="assemble",
    )(*pieces)


def unit_block(k, units):
    start = jnp.bitwise_xor(lax.axis_index("col"), k) * units
    return pl.ds(pl.multiple_of(start, units), units)


def span(i, size):
    return slice(i * size, (i + 1) * size)


def fetches(k, hbm, vmem, sems):
    units, width = vmem[2].shape
    mine = unit_block(k, units)
    part = width // CHUNKS
    copies = []
    for i in range(CHUNKS):
        rows = pl.ds(i * part, part)
        ends = [
            (hbm[0].at[rows, mine], vmem[0].at[rows]),
            (hbm[1].at[rows, mine], vmem[1].at[rows]),
            (hbm[2].at[mine, rows], vmem[2].at[:, rows]),
        ]
        copies.append(
            [pltpu.make_async_copy(*ends[j], sems.at[i, j]) for j in range(len(ends))]
        )
    return copies


def sums_kernel(k, tok, grad, gate_w, up_w, down_w, *refs):
    out, gate_b, up_b, down_b, sems, gate, up, back = refs[-8:]
    moves = (
        (gate, lambda here: dot(tok[:, here], gate_b[here])),
        (up, lambda here: dot(tok[:, here], up_b[here])),
        (back, lambda here: back_dot(grad[:, here], down_b[:, here])),
    )
    copies = fetches(k, (gate_w, up_w, down_w), (gate_b, up_b, down_b), sems)
    for chunk in copies:
        for copy in chunk:
            copy.start()
    part = grad.shape[1] // CHUNKS
    for i, chunk in enumerate(copies):
        here = span(i, part)
        for copy, (acc, term) in zip(chunk, moves):
            copy.wait()
            if i == 0:
                acc[...] = term(here)
            else:
                acc[...] += term(here)
    out[0] = gate[...].astype(out.dtype)
    out[1] = up[...].astype(out.dtype)
    out[2] = back[...].astype(out.dtype)


def partial_sums(k, tok, grad, weights, units, dtype):
    total, width = tok.shape
    shapes = [(width, units), (width, units), (units, width)]
    return pl.pallas_call(
        functools.partial(sums_kernel, k),
        in_specs=[WHOLE, WHOLE] + [HOLD] * 3,
        out_specs=[WHOLE] * 4,
        scratch_shapes=[pltpu.SemaphoreType.DMA((CHUNKS, 3))]
        + [pltpu.VMEM((total, units), F32)] * 3,
        out_shape=[array((3, total, units), dtype)] + [vmem_array(x) for x in shapes],
        compiler_params=PARAMS,
        cost_estimate=estimate(6 * total * width * units, 6 * width * units),
        name="partial_sums",
    )(tok, grad, *in_hbm(weights))


def combine_kernel(own, other, out):
    out[...] = (own[...] + other[...].astype(F32)).astype(BF16)


def combine(own, other):
    return pl.pallas_call(
        combine_kernel,
        out_shape=array(own.shape, BF16),
        compiler_params=PARAMS,
        cost_estimate=estimate(own.size, 8 * own.size),
        name="combine",
    )(own, other)


def activate_kernel(own, *refs):
    others, out = refs[:-1], refs[-1]
    gate, up, hidden_grad = (
        functools.reduce(lambda s, o: s + o[j].astype(F32), others, own[j]) for j in range(3)
    )
    sig = jax.nn.sigmoid(gate)
    swish = gate * sig
    out[0] = (swish * up).astype(BF16)
    out[1] = (hidden_grad * up * sig * (1.0 + gate * (1.0 - sig))).astype(BF16)
    out[2] = (hidden_grad * swish).astype(BF16)


def activate(own, others):
    return pl.pallas_call(
        activate_kernel,
        out_shape=array(own.shape, BF16),
        compiler_params=PARAMS,
        cost_estimate=estimate(8 * own.size, 12 * own.size),
        name="activate",
    )(own, *others)


def use_kernel(k, first, last, with_products, with_grads, act, *refs):
    refs = list(refs)
    leaving = []
    if with_products:
        gate_w, up_w, down_w = (refs.pop(0) for _ in range(3))
        before = None if first else refs.pop(0)
    if with_grads:
        tok_t, grad = refs.pop(0), refs.pop(0)
        gate_s, up_s, down_s, sems = refs[-4:]
        refs = refs[:-4]
        gate_g, up_g, down_g = refs[-3:]
        refs = refs[:-3]
        units, width = down_s.shape
        part, rows = width // CHUNKS, units // CHUNKS
        hidden_t = act[0].astype(F32).T.astype(BF16)
        mine = unit_block(k, units)
        start = jnp.bitwise_xor(lax.axis_index("col"), k) * units
        for i in range(CHUNKS):
            here, some = span(i, part), span(i, rows)
            gate_s[here] = dot(tok_t[here], act[1]).astype(BF16)
            up_s[here] = dot(tok_t[here], act[2]).astype(BF16)
            down_s[some] = dot(hidden_t[some], grad[...]).astype(BF16)
            there = pl.ds(i * part, part)
            below = pl.ds(pl.multiple_of(start + i * rows, rows), rows)
            ends = (
                (gate_s.at[there], gate_g.at[there, mine]),
                (up_s.at[there], up_g.at[there, mine]),
                (down_s.at[pl.ds(i * rows, rows)], down_g.at[below]),
            )
            for j, (source, target) in enumerate(ends):
                copy = pltpu.make_async_copy(source, target, sems.at[i, j])
                copy.start()
                leaving.append(copy)
    if with_products:
        outs = refs[-1 - last :]
        for i in range(down_w.shape[1] // PIECE):
            here = span(i, PIECE)
            back = back_dot(act[1], gate_w[here]) + back_dot(act[2], up_w[here])
            for j, term in enumerate((dot(act[0], down_w[:, here]), back)):
                term = term if first else before[j, :, here] + term
                if last:
                    half = term.shape[0] // 2
                    outs[0][j, :, here] = term[:half]
                    outs[1][j, :, here] = term[half:]
                else:
                    outs[0][j, :, here] = term
    for copy in leaving:
        copy.wait()


def use(k, act, weights=None, terms=None, last=False, sides=None, grads=(), after=()):
    _, total, units = act.shape
    first = terms is None
    specs, args = [WHOLE], [act]
    out_specs, out_shape, scratch, aliases = [], [], [], {}
    moved = 0
    if weights is not None:
        width = weights[2].shape[1]
        specs += [WHOLE] * 3
        args += in_vmem(weights)
        if not first:
            specs.append(WHOLE)
            args.append(terms)
        held = total // 2 if last else total
        out_specs += [WHOLE] * (1 + last)
        out_shape += [array((2, held, width), F32)] * (1 + last)
        moved += 6 * width * units
    if sides is not None:
        tok_t, grad, all_units = sides
        width = grad.shape[1]
        specs += [WHOLE, WHOLE]
        args += [tok_t, grad]
        for j, grad_before in enumerate(grads):
            aliases[len(args)] = len(out_shape) + j
            specs.append(HOLD)
            args.append(grad_before)
        out_specs += [HOLD] * 3
        out_shape += [pltpu.HBM((width, all_units), BF16)] * 2
        out_shape.append(pltpu.HBM((all_units, width), BF16))
        scratch += [pltpu.VMEM((width, units), BF16)] * 2
        scratch += [pltpu.VMEM((units, width), BF16), pltpu.SemaphoreType.DMA((CHUNKS, 3))]
        moved += 6 * width * units
    return pl.pallas_call(
        functools.partial(use_kernel, k, first, last, weights is not None, sides is not None),
        in_specs=specs + [HOLD] * len(after),
        out_specs=out_specs,
        scratch_shapes=scratch,
        out_shape=out_shape,
        input_output_aliases=aliases,
        compiler_params=PARAMS,
        cost_estimate=estimate(total * moved, moved),
        name=("products" if weights else "") + ("grads" if sides else ""),
    )(*args, *after)


def fold_kernel(rows, own, other, keep, *sent):
    total = own[...] + other[...]
    keep[...] = total[:, :rows]
    for i, out in enumerate(sent, 1):
        out[...] = total[:, i * rows : (i + 1) * rows].astype(BF16)


def fold(own, other, rows):
    _, total, width = own.shape
    others = total // rows - 1
    return pl.pallas_call(
        functools.partial(fold_kernel, rows),
        out_shape=[array((2, rows, width), F32)] + [array((2, rows, width), BF16)] * others,
        compiler_params=PARAMS,
        cost_estimate=estimate(own.size, 12 * own.size),
        name="fold",
    )(own, other)


def finish_kernel(own, *refs):
    others, outs = refs[:-2], refs[-2:]
    for j, out in enumerate(outs):
        total = functools.reduce(lambda s, o: s + o[j].astype(F32), others, own[j])
        out[...] = total.astype(BF16)


def finish(own, others):
    return pl.pallas_call(
        finish_kernel,
        out_shape=[array(own.shape[1:], BF16)] * 2,
        compiler_params=PARAMS,
        cost_estimate=estimate(own.size, 12 * own.size),
        name="finish",
    )(own, *others)


def pairwise(n_row, n_col, tokens, gate_weight, up_weight, down_weight, out_grad):
    rows = tokens.shape[0]
    all_units = gate_weight.shape[1]
    units = all_units // n_col
    weights = (gate_weight, up_weight, down_weight)
    along_row = functools.partial(swap, axis="row", size=n_row)
    along_col = functools.partial(swap, axis="col", size=n_col)

    mine = pack(tokens, out_grad)
    even = [mine] + [along_row(mine, k=k) for k in range(2, n_row, 2)]
    odd = [along_row(piece, k=1) for piece in even]
    tok, grad, tok_t = assemble(even + odd, rows)
    sides = (tok_t, grad, all_units)

    sums = functools.partial(partial_sums, tok=tok, grad=grad, weights=weights, units=units)
    there, *last_weights = sums(3, dtype=BF16)
    near = along_col(there, k=1)
    here, *far_weights = sums(2, dtype=F32)
    from_far = along_col(combine(here, near), k=2)
    there, *near_weights = sums(1, dtype=BF16)
    from_near = along_col(there, k=1)
    here, *own_weights = sums(0, dtype=F32)
    own = activate(here, [from_near, from_far])

    near_act = along_col(own, k=1)
    far_act = along_col(own, k=2)
    terms, *grads = use(0, own, own_weights, sides=sides)
    terms, *grads = use(1, near_act, near_weights, terms, sides=sides, grads=grads)
    held, _ = lax.optimization_barrier((far_act, (terms, grads)))
    last_act = along_col(held, k=1)
    terms, *grads = use(2, far_act, far_weights, terms, sides=sides, grads=grads)
    kept, given = use(3, last_act, last_weights, terms, last=True)

    other = along_row(given, k=1)
    mine, *sent = fold(kept, other, rows)
    parts = [along_row(piece, k=2 * i) for i, piece in enumerate(sent, 1)]
    grads = use(3, last_act, sides=sides, grads=grads, after=(mine,))
    mixed, input_grad = finish(mine, parts)
    return (mixed, input_grad, *grads)


def gathered(tokens, gate_weight, up_weight, down_weight, out_grad):
    tok = lax.all_gather(tokens, "row", axis=0, tiled=True)
    grad = lax.all_gather(out_grad, "row", axis=0, tiled=True)

    def total(x):
        return lax.psum_scatter(x, "col", scatter_dimension=0, tiled=True)

    def outer(a, b):
        return lax.dot_general(a, b, CONTRACT, preferred_element_type=F32).astype(BF16)

    gate, up = total(dot(tok, gate_weight)), total(dot(tok, up_weight))
    hidden_grad = total(back_dot(grad, down_weight))
    sig = jax.nn.sigmoid(gate)
    swish = gate * sig
    hidden = (swish * up).astype(BF16)
    gate_delta = (hidden_grad * up * sig * (1.0 + gate * (1.0 - sig))).astype(BF16)
    up_delta = (hidden_grad * swish).astype(BF16)
    hidden, gate_delta, up_delta = (
        lax.all_gather(x, "col", axis=0, tiled=True) for x in (hidden, gate_delta, up_delta)
    )
    mixed = dot(hidden, down_weight)
    input_grad = back_dot(gate_delta, gate_weight) + back_dot(up_delta, up_weight)
    mixed, input_grad = (
        lax.psum_scatter(x, "row", scatter_dimension=0, tiled=True).astype(BF16)
        for x in (mixed, input_grad)
    )
    return (
        mixed,
        input_grad,
        outer(tok, gate_delta),
        outer(tok, up_delta),
        outer(hidden, grad),
    )


def solution(mesh):
    n_row, n_col = mesh.shape["row"], mesh.shape["col"]

    def shards(*args):
        tokens, gate_weight = args[:2]
        fits = (
            n_row & (n_row - 1) == 0
            and n_row > 1
            and n_col == 4
            and tokens.shape[0] % 8 == 0
            and tokens.shape[1] % (128 * CHUNKS) == 0
            and gate_weight.shape[1] % (128 * n_col) == 0
            and gate_weight.shape[1] % (16 * CHUNKS * n_col) == 0
            and tokens.shape[1] % PIECE == 0
            and 6 * gate_weight.size <= 36 * 1024 * 1024
        )
        if fits:
            return pairwise(n_row, n_col, *args)
        return gathered(*args)

    return jax.shard_map(
        shards,
        mesh=mesh,
        in_specs=(
            P("row", "col"),
            P("col", "row"),
            P("col", "row"),
            P("row", "col"),
            P("row", "col"),
        ),
        out_specs=(
            P("row", "col"),
            P("row", "col"),
            P("col", "row"),
            P("col", "row"),
            P("row", "col"),
        ),
        check_vma=False,
    )
```

```python
import functools

import jax
import jax.numpy as jnp
from jax import lax
from jax.experimental import pallas as pl
from jax.experimental.pallas import tpu as pltpu
from jax.sharding import PartitionSpec as P

BF16 = jnp.bfloat16
F32 = jnp.float32
VMEM_LIMIT = 14 * 1024 * 1024
CHUNKS = 8
BACK = (((1,), (1,)), ((), ()))
CONTRACT = (((0,), (0,)), ((), ()))
PARAMS = pltpu.CompilerParams(vmem_limit_bytes=VMEM_LIMIT)
HOLD = pl.BlockSpec(memory_space=pl.ANY)
PIECE = 512
WHOLE = pl.BlockSpec(memory_space=pltpu.VMEM)


def dot(a, b):
    return jnp.dot(a, b, preferred_element_type=F32)


def back_dot(a, b):
    return lax.dot_general(a, b, BACK, preferred_element_type=F32)


def swap(x, axis, size, k):
    return lax.ppermute(x, axis, [(i, i ^ k) for i in range(size)])


def estimate(flops, num_bytes):
    return pl.CostEstimate(flops=flops // 8, bytes_accessed=num_bytes // 8, transcendentals=0)


def vmem_array(shape):
    return pltpu.VMEM(shape, BF16)


def in_vmem(arrays):
    return [pltpu.with_memory_space_constraint(x, pltpu.VMEM) for x in arrays]


def in_hbm(arrays):
    return [pltpu.with_memory_space_constraint(x, pltpu.HBM) for x in arrays]


def array(shape, dtype):
    return jax.ShapeDtypeStruct(shape, dtype)


def pack_kernel(tokens, out_grad, out):
    joined = jnp.concatenate([tokens[...].astype(F32), out_grad[...].astype(F32)], axis=0)
    out[...] = joined.astype(BF16)


def pack(tokens, out_grad):
    rows, width = tokens.shape
    return pl.pallas_call(
        pack_kernel,
        out_shape=array((2 * rows, width), BF16),
        compiler_params=PARAMS,
        cost_estimate=estimate(0, 8 * rows * width),
        name="pack",
    )(*in_hbm((tokens, out_grad)))


def assemble_kernel(rows, *refs):
    pieces, (tok, grad, tok_t) = refs[:-3], refs[-3:]
    both = [p[...].astype(F32) for p in pieces]
    all_tok = jnp.concatenate([b[:rows] for b in both], axis=0)
    all_grad = jnp.concatenate([b[rows:] for b in both], axis=0)
    tok[...] = all_tok.astype(BF16)
    grad[...] = all_grad.astype(BF16)
    tok_t[...] = all_tok.T.astype(BF16)


def assemble(pieces, rows):
    total, width = rows * len(pieces), pieces[0].shape[1]
    flat = (total, width)
    return pl.pallas_call(
        functools.partial(assemble_kernel, rows),
        out_shape=[array(shape, BF16) for shape in (flat, flat, (width, total))],
        compiler_params=PARAMS,
        cost_estimate=estimate(0, 12 * total * width),
        name="assemble",
    )(*pieces)


def unit_block(k, units):
    start = jnp.bitwise_xor(lax.axis_index("col"), k) * units
    return pl.ds(pl.multiple_of(start, units), units)


def span(i, size):
    return slice(i * size, (i + 1) * size)


def fetches(k, hbm, vmem, sems):
    units, width = vmem[2].shape
    mine = unit_block(k, units)
    part = width // CHUNKS
    copies = []
    for i in range(CHUNKS):
        rows = pl.ds(i * part, part)
        ends = [
            (hbm[0].at[rows, mine], vmem[0].at[rows]),
            (hbm[1].at[rows, mine], vmem[1].at[rows]),
            (hbm[2].at[mine, rows], vmem[2].at[:, rows]),
        ]
        copies.append(
            [pltpu.make_async_copy(*ends[j], sems.at[i, j]) for j in range(len(ends))]
        )
    return copies


def block_shapes(units, width):
    return [(width, units), (width, units), (units, width)]


def load_kernel(k, *refs):
    copies = sum(fetches(k, refs[:3], refs[3:6], refs[6]), [])
    for copy in copies:
        copy.start()
    for copy in copies:
        copy.wait()


def load(k, weights, units):
    shapes = block_shapes(units, weights[0].shape[0])
    return pl.pallas_call(
        functools.partial(load_kernel, k),
        in_specs=[HOLD] * 3,
        out_specs=[WHOLE] * 3,
        scratch_shapes=[pltpu.SemaphoreType.DMA((CHUNKS, 3))],
        out_shape=[vmem_array(x) for x in shapes],
        compiler_params=PARAMS,
        cost_estimate=estimate(0, 6 * weights[0].shape[0] * units),
        name="load",
    )(*in_hbm(weights))


def sums_kernel(following, tok, grad, gate_b, up_b, down_b, *refs):
    copies = []
    if following is not None:
        hbm, out, kept, sems = refs[:3], refs[3], refs[4:7], refs[7]
        copies = sum(fetches(following, hbm, kept, sems), [])
    else:
        (out,) = refs
    for copy in copies:
        copy.start()
    out[0] = dot(tok[...], gate_b[...]).astype(out.dtype)
    out[1] = dot(tok[...], up_b[...]).astype(out.dtype)
    out[2] = back_dot(grad[...], down_b[...]).astype(out.dtype)
    for copy in copies:
        copy.wait()


def partial_sums(block, tok, grad, dtype, weights=None, following=None):
    total, width = tok.shape
    units = block[2].shape[0]
    more = following is not None
    shapes = block_shapes(units, width) if more else []
    return pl.pallas_call(
        functools.partial(sums_kernel, following),
        in_specs=[WHOLE] * 5 + [HOLD] * (3 * more),
        out_specs=[WHOLE] * (1 + 3 * more),
        scratch_shapes=[pltpu.SemaphoreType.DMA((CHUNKS, 3))] * more,
        out_shape=[array((3, total, units), dtype)] + [vmem_array(x) for x in shapes],
        compiler_params=PARAMS,
        cost_estimate=estimate(6 * total * width * units, 6 * width * units),
        name="partial_sums",
    )(tok, grad, *in_vmem(block), *(in_hbm(weights) if more else ()))


def combine_kernel(own, other, out):
    out[...] = (own[...] + other[...].astype(F32)).astype(BF16)


def combine(own, other):
    return pl.pallas_call(
        combine_kernel,
        out_shape=array(own.shape, BF16),
        compiler_params=PARAMS,
        cost_estimate=estimate(own.size, 8 * own.size),
        name="combine",
    )(own, other)


def activate_kernel(own, *refs):
    others, out = refs[:-1], refs[-1]
    gate, up, hidden_grad = (
        functools.reduce(lambda s, o: s + o[j].astype(F32), others, own[j]) for j in range(3)
    )
    sig = jax.nn.sigmoid(gate)
    swish = gate * sig
    out[0] = (swish * up).astype(BF16)
    out[1] = (hidden_grad * up * sig * (1.0 + gate * (1.0 - sig))).astype(BF16)
    out[2] = (hidden_grad * swish).astype(BF16)


def activate(own, others):
    return pl.pallas_call(
        activate_kernel,
        out_shape=array(own.shape, BF16),
        compiler_params=PARAMS,
        cost_estimate=estimate(8 * own.size, 12 * own.size),
        name="activate",
    )(own, *others)


def use_kernel(k, first, last, with_products, with_grads, act, *refs):
    refs = list(refs)
    leaving = []
    if with_products:
        gate_w, up_w, down_w = (refs.pop(0) for _ in range(3))
        before = None if first else refs.pop(0)
    if with_grads:
        tok_t, grad = refs.pop(0), refs.pop(0)
        gate_s, up_s, down_s, sems = refs[-4:]
        refs = refs[:-4]
        gate_g, up_g, down_g = refs[-3:]
        refs = refs[:-3]
        units, width = down_s.shape
        part, rows = width // CHUNKS, units // CHUNKS
        hidden_t = act[0].astype(F32).T.astype(BF16)
        mine = unit_block(k, units)
        start = jnp.bitwise_xor(lax.axis_index("col"), k) * units
        for i in range(CHUNKS):
            here, some = span(i, part), span(i, rows)
            gate_s[here] = dot(tok_t[here], act[1]).astype(BF16)
            up_s[here] = dot(tok_t[here], act[2]).astype(BF16)
            down_s[some] = dot(hidden_t[some], grad[...]).astype(BF16)
            there = pl.ds(i * part, part)
            below = pl.ds(pl.multiple_of(start + i * rows, rows), rows)
            ends = (
                (gate_s.at[there], gate_g.at[there, mine]),
                (up_s.at[there], up_g.at[there, mine]),
                (down_s.at[pl.ds(i * rows, rows)], down_g.at[below]),
            )
            for j, (source, target) in enumerate(ends):
                copy = pltpu.make_async_copy(source, target, sems.at[i, j])
                copy.start()
                leaving.append(copy)
    if with_products:
        outs = refs[-1 - last :]
        for i in range(down_w.shape[1] // PIECE):
            here = span(i, PIECE)
            back = back_dot(act[1], gate_w[here]) + back_dot(act[2], up_w[here])
            for j, term in enumerate((dot(act[0], down_w[:, here]), back)):
                term = term if first else before[j, :, here] + term
                if last:
                    half = term.shape[0] // 2
                    outs[0][j, :, here] = term[:half]
                    outs[1][j, :, here] = term[half:]
                else:
                    outs[0][j, :, here] = term
    for copy in leaving:
        copy.wait()


def use(k, act, weights=None, terms=None, last=False, sides=None, grads=(), after=()):
    _, total, units = act.shape
    first = terms is None
    specs, args = [WHOLE], [act]
    out_specs, out_shape, scratch, aliases = [], [], [], {}
    moved = 0
    if weights is not None:
        width = weights[2].shape[1]
        specs += [WHOLE] * 3
        args += in_vmem(weights)
        if not first:
            specs.append(WHOLE)
            args.append(terms)
        held = total // 2 if last else total
        out_specs += [WHOLE] * (1 + last)
        out_shape += [array((2, held, width), F32)] * (1 + last)
        moved += 6 * width * units
    if sides is not None:
        tok_t, grad, all_units = sides
        width = grad.shape[1]
        specs += [WHOLE, WHOLE]
        args += [tok_t, grad]
        for j, grad_before in enumerate(grads):
            aliases[len(args)] = len(out_shape) + j
            specs.append(HOLD)
            args.append(grad_before)
        out_specs += [HOLD] * 3
        out_shape += [pltpu.HBM((width, all_units), BF16)] * 2
        out_shape.append(pltpu.HBM((all_units, width), BF16))
        scratch += [pltpu.VMEM((width, units), BF16)] * 2
        scratch += [pltpu.VMEM((units, width), BF16), pltpu.SemaphoreType.DMA((CHUNKS, 3))]
        moved += 6 * width * units
    return pl.pallas_call(
        functools.partial(use_kernel, k, first, last, weights is not None, sides is not None),
        in_specs=specs + [HOLD] * len(after),
        out_specs=out_specs,
        scratch_shapes=scratch,
        out_shape=out_shape,
        input_output_aliases=aliases,
        compiler_params=PARAMS,
        cost_estimate=estimate(total * moved, moved),
        name=("products" if weights else "") + ("grads" if sides else ""),
    )(*args, *after)


def fold_kernel(rows, own, other, keep, *sent):
    total = own[...] + other[...]
    keep[...] = total[:, :rows]
    for i, out in enumerate(sent, 1):
        out[...] = total[:, i * rows : (i + 1) * rows].astype(BF16)


def fold(own, other, rows):
    _, total, width = own.shape
    others = total // rows - 1
    return pl.pallas_call(
        functools.partial(fold_kernel, rows),
        out_shape=[array((2, rows, width), F32)] + [array((2, rows, width), BF16)] * others,
        compiler_params=PARAMS,
        cost_estimate=estimate(own.size, 12 * own.size),
        name="fold",
    )(own, other)


def finish_kernel(own, *refs):
    others, outs = refs[:-2], refs[-2:]
    for j, out in enumerate(outs):
        total = functools.reduce(lambda s, o: s + o[j].astype(F32), others, own[j])
        out[...] = total.astype(BF16)


def finish(own, others):
    return pl.pallas_call(
        finish_kernel,
        out_shape=[array(own.shape[1:], BF16)] * 2,
        compiler_params=PARAMS,
        cost_estimate=estimate(own.size, 12 * own.size),
        name="finish",
    )(own, *others)


def pairwise(n_row, n_col, tokens, gate_weight, up_weight, down_weight, out_grad):
    rows = tokens.shape[0]
    all_units = gate_weight.shape[1]
    units = all_units // n_col
    weights = (gate_weight, up_weight, down_weight)
    along_row = functools.partial(swap, axis="row", size=n_row)
    along_col = functools.partial(swap, axis="col", size=n_col)

    mine = pack(tokens, out_grad)
    last_weights = load(3, weights, units)
    away = [along_row(mine, k=k) for k in range(2, n_row, 2)]
    away, last_weights = lax.optimization_barrier((away, last_weights))
    even = [mine, *away]
    odd = [along_row(piece, k=1) for piece in even]
    tok, grad, tok_t = assemble(even + odd, rows)
    sides = (tok_t, grad, all_units)

    there, *near_weights = partial_sums(last_weights, tok, grad, BF16, weights, 1)
    near = along_col(there, k=1)
    there, *far_weights = partial_sums(near_weights, tok, grad, BF16, weights, 2)
    from_near = along_col(there, k=1)
    here, *own_weights = partial_sums(far_weights, tok, grad, F32, weights, 0)
    from_far = along_col(combine(here, near), k=2)
    (here,) = partial_sums(own_weights, tok, grad, F32)
    own = activate(here, [from_near, from_far])

    near_act = along_col(own, k=1)
    far_act = along_col(own, k=2)
    terms, *grads = use(0, own, own_weights, sides=sides)
    held, _ = lax.optimization_barrier((far_act, (terms, grads)))
    last_act = along_col(held, k=1)
    terms, *grads = use(1, near_act, near_weights, terms, sides=sides, grads=grads)
    terms, *grads = use(2, far_act, far_weights, terms, sides=sides, grads=grads)
    kept, given = use(3, last_act, last_weights, terms, last=True)

    other = along_row(given, k=1)
    mine, *sent = fold(kept, other, rows)
    parts = [along_row(piece, k=2 * i) for i, piece in enumerate(sent, 1)]
    grads = use(3, last_act, sides=sides, grads=grads, after=(mine,))
    mixed, input_grad = finish(mine, parts)
    return (mixed, input_grad, *grads)


def gathered(tokens, gate_weight, up_weight, down_weight, out_grad):
    tok = lax.all_gather(tokens, "row", axis=0, tiled=True)
    grad = lax.all_gather(out_grad, "row", axis=0, tiled=True)

    def total(x):
        return lax.psum_scatter(x, "col", scatter_dimension=0, tiled=True)

    def outer(a, b):
        return lax.dot_general(a, b, CONTRACT, preferred_element_type=F32).astype(BF16)

    gate, up = total(dot(tok, gate_weight)), total(dot(tok, up_weight))
    hidden_grad = total(back_dot(grad, down_weight))
    sig = jax.nn.sigmoid(gate)
    swish = gate * sig
    hidden = (swish * up).astype(BF16)
    gate_delta = (hidden_grad * up * sig * (1.0 + gate * (1.0 - sig))).astype(BF16)
    up_delta = (hidden_grad * swish).astype(BF16)
    hidden, gate_delta, up_delta = (
        lax.all_gather(x, "col", axis=0, tiled=True) for x in (hidden, gate_delta, up_delta)
    )
    mixed = dot(hidden, down_weight)
    input_grad = back_dot(gate_delta, gate_weight) + back_dot(up_delta, up_weight)
    mixed, input_grad = (
        lax.psum_scatter(x, "row", scatter_dimension=0, tiled=True).astype(BF16)
        for x in (mixed, input_grad)
    )
    return (
        mixed,
        input_grad,
        outer(tok, gate_delta),
        outer(tok, up_delta),
        outer(hidden, grad),
    )


def solution(mesh):
    n_row, n_col = mesh.shape["row"], mesh.shape["col"]

    def shards(*args):
        tokens, gate_weight = args[:2]
        fits = (
            n_row & (n_row - 1) == 0
            and n_row > 1
            and n_col == 4
            and tokens.shape[0] % 8 == 0
            and tokens.shape[1] % (128 * CHUNKS) == 0
            and gate_weight.shape[1] % (128 * n_col) == 0
            and gate_weight.shape[1] % (16 * CHUNKS * n_col) == 0
            and tokens.shape[1] % PIECE == 0
            and 6 * gate_weight.size <= 36 * 1024 * 1024
        )
        if fits:
            return pairwise(n_row, n_col, *args)
        return gathered(*args)

    return jax.shard_map(
        shards,
        mesh=mesh,
        in_specs=(
            P("row", "col"),
            P("col", "row"),
            P("col", "row"),
            P("row", "col"),
            P("row", "col"),
        ),
        out_specs=(
            P("row", "col"),
            P("row", "col"),
            P("col", "row"),
            P("col", "row"),
            P("row", "col"),
        ),
        check_vma=False,
    )
```

```python
import functools

import jax
import jax.numpy as jnp
from jax import lax
from jax.experimental import pallas as pl
from jax.experimental.pallas import tpu as pltpu
from jax.sharding import PartitionSpec as P

BF16 = jnp.bfloat16
F32 = jnp.float32
VMEM_LIMIT = 14 * 1024 * 1024
CHUNKS = 8
BACK = (((1,), (1,)), ((), ()))
CONTRACT = (((0,), (0,)), ((), ()))
PARAMS = pltpu.CompilerParams(vmem_limit_bytes=VMEM_LIMIT)
HOLD = pl.BlockSpec(memory_space=pl.ANY)
PIECE = 512
WHOLE = pl.BlockSpec(memory_space=pltpu.VMEM)


def dot(a, b):
    return jnp.dot(a, b, preferred_element_type=F32)


def back_dot(a, b):
    return lax.dot_general(a, b, BACK, preferred_element_type=F32)


def swap(x, axis, size, k):
    return lax.ppermute(x, axis, [(i, i ^ k) for i in range(size)])


def estimate(flops, num_bytes):
    return pl.CostEstimate(flops=flops // 8, bytes_accessed=num_bytes // 8, transcendentals=0)


def vmem_array(shape):
    return pltpu.VMEM(shape, BF16)


def in_vmem(arrays):
    return [pltpu.with_memory_space_constraint(x, pltpu.VMEM) for x in arrays]


def in_hbm(arrays):
    return [pltpu.with_memory_space_constraint(x, pltpu.HBM) for x in arrays]


def array(shape, dtype):
    return jax.ShapeDtypeStruct(shape, dtype)


def pack_kernel(tokens, out_grad, out):
    joined = jnp.concatenate([tokens[...].astype(F32), out_grad[...].astype(F32)], axis=0)
    out[...] = joined.astype(BF16)


def pack(tokens, out_grad):
    rows, width = tokens.shape
    return pl.pallas_call(
        pack_kernel,
        out_shape=array((2 * rows, width), BF16),
        compiler_params=PARAMS,
        cost_estimate=estimate(0, 8 * rows * width),
        name="pack",
    )(*in_hbm((tokens, out_grad)))


def assemble_kernel(rows, *refs):
    pieces, (tok, grad, tok_t) = refs[:-3], refs[-3:]
    both = [p[...].astype(F32) for p in pieces]
    all_tok = jnp.concatenate([b[:rows] for b in both], axis=0)
    all_grad = jnp.concatenate([b[rows:] for b in both], axis=0)
    tok[...] = all_tok.astype(BF16)
    grad[...] = all_grad.astype(BF16)
    tok_t[...] = all_tok.T.astype(BF16)


def assemble(pieces, rows):
    total, width = rows * len(pieces), pieces[0].shape[1]
    flat = (total, width)
    return pl.pallas_call(
        functools.partial(assemble_kernel, rows),
        out_shape=[array(shape, BF16) for shape in (flat, flat, (width, total))],
        compiler_params=PARAMS,
        cost_estimate=estimate(0, 12 * total * width),
        name="assemble",
    )(*pieces)


def unit_block(k, units):
    start = jnp.bitwise_xor(lax.axis_index("col"), k) * units
    return pl.ds(pl.multiple_of(start, units), units)


def span(i, size):
    return slice(i * size, (i + 1) * size)


def fetches(k, hbm, vmem, sems):
    units, width = vmem[2].shape
    mine = unit_block(k, units)
    part = width // CHUNKS
    copies = []
    for i in range(CHUNKS):
        rows = pl.ds(i * part, part)
        ends = [
            (hbm[0].at[rows, mine], vmem[0].at[rows]),
            (hbm[1].at[rows, mine], vmem[1].at[rows]),
            (hbm[2].at[mine, rows], vmem[2].at[:, rows]),
        ]
        copies.append(
            [pltpu.make_async_copy(*ends[j], sems.at[i, j]) for j in range(len(ends))]
        )
    return copies


def sums_kernel(k, tok, grad, gate_w, up_w, down_w, *refs):
    out, gate_b, up_b, down_b, sems, gate, up, back = refs[-8:]
    moves = (
        (gate, lambda here: dot(tok[:, here], gate_b[here])),
        (up, lambda here: dot(tok[:, here], up_b[here])),
        (back, lambda here: back_dot(grad[:, here], down_b[:, here])),
    )
    copies = fetches(k, (gate_w, up_w, down_w), (gate_b, up_b, down_b), sems)
    for chunk in copies:
        for copy in chunk:
            copy.start()
    part = grad.shape[1] // CHUNKS
    for i, chunk in enumerate(copies):
        here = span(i, part)
        for copy, (acc, term) in zip(chunk, moves):
            copy.wait()
            if i == 0:
                acc[...] = term(here)
            else:
                acc[...] += term(here)
    out[0] = gate[...].astype(out.dtype)
    out[1] = up[...].astype(out.dtype)
    out[2] = back[...].astype(out.dtype)


def partial_sums(k, tok, grad, weights, units, dtype, after=()):
    total, width = tok.shape
    shapes = [(width, units), (width, units), (units, width)]
    return pl.pallas_call(
        functools.partial(sums_kernel, k),
        in_specs=[WHOLE, WHOLE] + [HOLD] * (3 + len(after)),
        out_specs=[WHOLE] * 4,
        scratch_shapes=[pltpu.SemaphoreType.DMA((CHUNKS, 3))]
        + [pltpu.VMEM((total, units), F32)] * 3,
        out_shape=[array((3, total, units), dtype)] + [vmem_array(x) for x in shapes],
        compiler_params=PARAMS,
        cost_estimate=estimate(6 * total * width * units, 6 * width * units),
        name="partial_sums",
    )(tok, grad, *in_hbm(weights), *after)


def combine_kernel(own, other, out, token):
    token[...] = jnp.zeros_like(token)
    out[...] = (own[...] + other[...].astype(F32)).astype(BF16)


def combine(own, other):
    return pl.pallas_call(
        combine_kernel,
        out_shape=[array(own.shape, BF16), array((8, 128), F32)],
        compiler_params=PARAMS,
        cost_estimate=estimate(own.size, 8 * own.size),
        name="combine",
    )(own, other)


def activate_kernel(own, *refs):
    others, out = refs[:-1], refs[-1]
    gate, up, hidden_grad = (
        functools.reduce(lambda s, o: s + o[j].astype(F32), others, own[j]) for j in range(3)
    )
    sig = jax.nn.sigmoid(gate)
    swish = gate * sig
    out[0] = (swish * up).astype(BF16)
    out[1] = (hidden_grad * up * sig * (1.0 + gate * (1.0 - sig))).astype(BF16)
    out[2] = (hidden_grad * swish).astype(BF16)


def activate(own, others):
    return pl.pallas_call(
        activate_kernel,
        out_shape=array(own.shape, BF16),
        compiler_params=PARAMS,
        cost_estimate=estimate(8 * own.size, 12 * own.size),
        name="activate",
    )(own, *others)


def use_kernel(k, first, last, with_products, with_grads, act, *refs):
    refs = list(refs)
    leaving = []
    if with_products:
        gate_w, up_w, down_w = (refs.pop(0) for _ in range(3))
        before = None if first else refs.pop(0)
    if with_grads:
        tok_t, grad = refs.pop(0), refs.pop(0)
        gate_s, up_s, down_s, sems = refs[-4:]
        refs = refs[:-4]
        gate_g, up_g, down_g = refs[-3:]
        refs = refs[:-3]
        units, width = down_s.shape
        part, rows = width // CHUNKS, units // CHUNKS
        hidden_t = act[0].astype(F32).T.astype(BF16)
        mine = unit_block(k, units)
        start = jnp.bitwise_xor(lax.axis_index("col"), k) * units
        for i in range(CHUNKS):
            here, some = span(i, part), span(i, rows)
            gate_s[here] = dot(tok_t[here], act[1]).astype(BF16)
            up_s[here] = dot(tok_t[here], act[2]).astype(BF16)
            down_s[some] = dot(hidden_t[some], grad[...]).astype(BF16)
            there = pl.ds(i * part, part)
            below = pl.ds(pl.multiple_of(start + i * rows, rows), rows)
            ends = (
                (gate_s.at[there], gate_g.at[there, mine]),
                (up_s.at[there], up_g.at[there, mine]),
                (down_s.at[pl.ds(i * rows, rows)], down_g.at[below]),
            )
            for j, (source, target) in enumerate(ends):
                copy = pltpu.make_async_copy(source, target, sems.at[i, j])
                copy.start()
                leaving.append(copy)
    if with_products:
        outs = refs[-1 - last :]
        for i in range(down_w.shape[1] // PIECE):
            here = span(i, PIECE)
            back = back_dot(act[1], gate_w[here]) + back_dot(act[2], up_w[here])
            for j, term in enumerate((dot(act[0], down_w[:, here]), back)):
                term = term if first else before[j, :, here] + term
                if last:
                    half = term.shape[0] // 2
                    outs[0][j, :, here] = term[:half]
                    outs[1][j, :, here] = term[half:]
                else:
                    outs[0][j, :, here] = term
    for copy in leaving:
        copy.wait()


def use(k, act, weights=None, terms=None, last=False, sides=None, grads=(), after=()):
    _, total, units = act.shape
    first = terms is None
    specs, args = [WHOLE], [act]
    out_specs, out_shape, scratch, aliases = [], [], [], {}
    moved = 0
    if weights is not None:
        width = weights[2].shape[1]
        specs += [WHOLE] * 3
        args += in_vmem(weights)
        if not first:
            specs.append(WHOLE)
            args.append(terms)
        held = total // 2 if last else total
        out_specs += [WHOLE] * (1 + last)
        out_shape += [array((2, held, width), F32)] * (1 + last)
        moved += 6 * width * units
    if sides is not None:
        tok_t, grad, all_units = sides
        width = grad.shape[1]
        specs += [WHOLE, WHOLE]
        args += [tok_t, grad]
        for j, grad_before in enumerate(grads):
            aliases[len(args)] = len(out_shape) + j
            specs.append(HOLD)
            args.append(grad_before)
        out_specs += [HOLD] * 3
        out_shape += [pltpu.HBM((width, all_units), BF16)] * 2
        out_shape.append(pltpu.HBM((all_units, width), BF16))
        scratch += [pltpu.VMEM((width, units), BF16)] * 2
        scratch += [pltpu.VMEM((units, width), BF16), pltpu.SemaphoreType.DMA((CHUNKS, 3))]
        moved += 6 * width * units
    return pl.pallas_call(
        functools.partial(use_kernel, k, first, last, weights is not None, sides is not None),
        in_specs=specs + [HOLD] * len(after),
        out_specs=out_specs,
        scratch_shapes=scratch,
        out_shape=out_shape,
        input_output_aliases=aliases,
        compiler_params=PARAMS,
        cost_estimate=estimate(total * moved, moved),
        name=("products" if weights else "") + ("grads" if sides else ""),
    )(*args, *after)


def fold_kernel(rows, own, other, keep, *sent):
    total = own[...] + other[...]
    keep[...] = total[:, :rows]
    for i, out in enumerate(sent, 1):
        out[...] = total[:, i * rows : (i + 1) * rows].astype(BF16)


def fold(own, other, rows):
    _, total, width = own.shape
    others = total // rows - 1
    return pl.pallas_call(
        functools.partial(fold_kernel, rows),
        out_shape=[array((2, rows, width), F32)] + [array((2, rows, width), BF16)] * others,
        compiler_params=PARAMS,
        cost_estimate=estimate(own.size, 12 * own.size),
        name="fold",
    )(own, other)


def finish_kernel(own, *refs):
    others, outs = refs[:-2], refs[-2:]
    for j, out in enumerate(outs):
        total = functools.reduce(lambda s, o: s + o[j].astype(F32), others, own[j])
        out[...] = total.astype(BF16)


def finish(own, others):
    return pl.pallas_call(
        finish_kernel,
        out_shape=[array(own.shape[1:], BF16)] * 2,
        compiler_params=PARAMS,
        cost_estimate=estimate(own.size, 12 * own.size),
        name="finish",
    )(own, *others)


def pairwise(n_row, n_col, tokens, gate_weight, up_weight, down_weight, out_grad):
    rows = tokens.shape[0]
    all_units = gate_weight.shape[1]
    units = all_units // n_col
    weights = (gate_weight, up_weight, down_weight)
    along_row = functools.partial(swap, axis="row", size=n_row)
    along_col = functools.partial(swap, axis="col", size=n_col)

    mine = pack(tokens, out_grad)
    even = [mine] + [along_row(mine, k=k) for k in range(2, n_row, 2)]
    odd = [along_row(piece, k=1) for piece in even]
    tok, grad, tok_t = assemble(even + odd, rows)
    sides = (tok_t, grad, all_units)

    sums = functools.partial(partial_sums, tok=tok, grad=grad, weights=weights, units=units)
    there, *last_weights = sums(3, dtype=BF16)
    near = along_col(there, k=1)
    here, *far_weights = sums(2, dtype=F32)
    pair, token = combine(here, near)
    from_far = along_col(pair, k=2)
    there, *near_weights = sums(1, dtype=BF16, after=(token,))
    from_near = along_col(there, k=1)
    here, *own_weights = sums(0, dtype=F32)
    own = activate(here, [from_near, from_far])

    near_act = along_col(own, k=1)
    (terms,) = use(0, own, own_weights)
    held, _ = lax.optimization_barrier((own, terms))
    far_act = along_col(held, k=2)
    grads = use(0, held, sides=sides)
    terms, *grads = use(1, near_act, near_weights, terms, sides=sides, grads=grads)
    held, _ = lax.optimization_barrier((far_act, (terms, grads)))
    last_act = along_col(held, k=1)
    terms, *grads = use(2, far_act, far_weights, terms, sides=sides, grads=grads)
    kept, given = use(3, last_act, last_weights, terms, last=True)

    other = along_row(given, k=1)
    mine, *sent = fold(kept, other, rows)
    parts = [along_row(piece, k=2 * i) for i, piece in enumerate(sent, 1)]
    grads = use(3, last_act, sides=sides, grads=grads, after=(mine,))
    mixed, input_grad = finish(mine, parts)
    return (mixed, input_grad, *grads)


def gathered(tokens, gate_weight, up_weight, down_weight, out_grad):
    tok = lax.all_gather(tokens, "row", axis=0, tiled=True)
    grad = lax.all_gather(out_grad, "row", axis=0, tiled=True)

    def total(x):
        return lax.psum_scatter(x, "col", scatter_dimension=0, tiled=True)

    def outer(a, b):
        return lax.dot_general(a, b, CONTRACT, preferred_element_type=F32).astype(BF16)

    gate, up = total(dot(tok, gate_weight)), total(dot(tok, up_weight))
    hidden_grad = total(back_dot(grad, down_weight))
    sig = jax.nn.sigmoid(gate)
    swish = gate * sig
    hidden = (swish * up).astype(BF16)
    gate_delta = (hidden_grad * up * sig * (1.0 + gate * (1.0 - sig))).astype(BF16)
    up_delta = (hidden_grad * swish).astype(BF16)
    hidden, gate_delta, up_delta = (
        lax.all_gather(x, "col", axis=0, tiled=True) for x in (hidden, gate_delta, up_delta)
    )
    mixed = dot(hidden, down_weight)
    input_grad = back_dot(gate_delta, gate_weight) + back_dot(up_delta, up_weight)
    mixed, input_grad = (
        lax.psum_scatter(x, "row", scatter_dimension=0, tiled=True).astype(BF16)
        for x in (mixed, input_grad)
    )
    return (
        mixed,
        input_grad,
        outer(tok, gate_delta),
        outer(tok, up_delta),
        outer(hidden, grad),
    )


def solution(mesh):
    n_row, n_col = mesh.shape["row"], mesh.shape["col"]

    def shards(*args):
        tokens, gate_weight = args[:2]
        fits = (
            n_row & (n_row - 1) == 0
            and n_row > 1
            and n_col == 4
            and tokens.shape[0] % 8 == 0
            and tokens.shape[1] % (128 * CHUNKS) == 0
            and gate_weight.shape[1] % (128 * n_col) == 0
            and gate_weight.shape[1] % (16 * CHUNKS * n_col) == 0
            and tokens.shape[1] % PIECE == 0
            and 6 * gate_weight.size <= 36 * 1024 * 1024
        )
        if fits:
            return pairwise(n_row, n_col, *args)
        return gathered(*args)

    return jax.shard_map(
        shards,
        mesh=mesh,
        in_specs=(
            P("row", "col"),
            P("col", "row"),
            P("col", "row"),
            P("row", "col"),
            P("row", "col"),
        ),
        out_specs=(
            P("row", "col"),
            P("row", "col"),
            P("col", "row"),
            P("col", "row"),
            P("row", "col"),
        ),
        check_vma=False,
    )
```

```python
import functools

import jax
import jax.numpy as jnp
from jax import lax
from jax.experimental import pallas as pl
from jax.experimental.pallas import tpu as pltpu
from jax.sharding import PartitionSpec as P

BF16 = jnp.bfloat16
F32 = jnp.float32
VMEM_LIMIT = 14 * 1024 * 1024
CHUNKS = 8
FETCHES = 4
BACK = (((1,), (1,)), ((), ()))
CONTRACT = (((0,), (0,)), ((), ()))
PARAMS = pltpu.CompilerParams(vmem_limit_bytes=VMEM_LIMIT)
HOLD = pl.BlockSpec(memory_space=pl.ANY)
PIECE = 512
WHOLE = pl.BlockSpec(memory_space=pltpu.VMEM)


def dot(a, b):
    return jnp.dot(a, b, preferred_element_type=F32)


def back_dot(a, b):
    return lax.dot_general(a, b, BACK, preferred_element_type=F32)


def swap(x, axis, size, k):
    return lax.ppermute(x, axis, [(i, i ^ k) for i in range(size)])


def estimate(flops, num_bytes):
    return pl.CostEstimate(flops=flops // 8, bytes_accessed=num_bytes // 8, transcendentals=0)


def vmem_array(shape):
    return pltpu.VMEM(shape, BF16)


def in_vmem(arrays):
    return [pltpu.with_memory_space_constraint(x, pltpu.VMEM) for x in arrays]


def in_hbm(arrays):
    return [pltpu.with_memory_space_constraint(x, pltpu.HBM) for x in arrays]


def array(shape, dtype):
    return jax.ShapeDtypeStruct(shape, dtype)


def pack_kernel(tokens, out_grad, out):
    joined = jnp.concatenate([tokens[...].astype(F32), out_grad[...].astype(F32)], axis=0)
    out[...] = joined.astype(BF16)


def pack(tokens, out_grad):
    rows, width = tokens.shape
    return pl.pallas_call(
        pack_kernel,
        out_shape=array((2 * rows, width), BF16),
        compiler_params=PARAMS,
        cost_estimate=estimate(0, 8 * rows * width),
        name="pack",
    )(*in_hbm((tokens, out_grad)))


def assemble_kernel(rows, *refs):
    pieces, (tok, grad, tok_t) = refs[:-3], refs[-3:]
    both = [p[...].astype(F32) for p in pieces]
    all_tok = jnp.concatenate([b[:rows] for b in both], axis=0)
    all_grad = jnp.concatenate([b[rows:] for b in both], axis=0)
    tok[...] = all_tok.astype(BF16)
    grad[...] = all_grad.astype(BF16)
    tok_t[...] = all_tok.T.astype(BF16)


def assemble(pieces, rows):
    total, width = rows * len(pieces), pieces[0].shape[1]
    flat = (total, width)
    return pl.pallas_call(
        functools.partial(assemble_kernel, rows),
        out_shape=[array(shape, BF16) for shape in (flat, flat, (width, total))],
        compiler_params=PARAMS,
        cost_estimate=estimate(0, 12 * total * width),
        name="assemble",
    )(*pieces)


def unit_block(k, units):
    start = jnp.bitwise_xor(lax.axis_index("col"), k) * units
    return pl.ds(pl.multiple_of(start, units), units)


def span(i, size):
    return slice(i * size, (i + 1) * size)


def fetches(k, hbm, vmem, sems):
    units, width = vmem[2].shape
    mine = unit_block(k, units)
    start = jnp.bitwise_xor(lax.axis_index("col"), k) * units
    tall, wide = width // FETCHES, units // FETCHES
    copies = []
    for i in range(FETCHES):
        rows, some = pl.ds(i * tall, tall), pl.ds(i * wide, wide)
        below = pl.ds(pl.multiple_of(start + i * wide, wide), wide)
        ends = (
            (hbm[0].at[rows, mine], vmem[0].at[rows]),
            (hbm[1].at[rows, mine], vmem[1].at[rows]),
            (hbm[2].at[below], vmem[2].at[some]),
        )
        copies += [pltpu.make_async_copy(*ends[j], sems.at[i, j]) for j in range(3)]
    return copies


def block_shapes(units, width):
    return [(width, units), (width, units), (units, width)]


def load_kernel(k, *refs):
    copies = fetches(k, refs[:3], refs[3:6], refs[6])
    for copy in copies:
        copy.start()
    for copy in copies:
        copy.wait()


def load(k, weights, units):
    shapes = block_shapes(units, weights[0].shape[0])
    return pl.pallas_call(
        functools.partial(load_kernel, k),
        in_specs=[HOLD] * 3,
        out_specs=[WHOLE] * 3,
        scratch_shapes=[pltpu.SemaphoreType.DMA((FETCHES, 3))],
        out_shape=[vmem_array(x) for x in shapes],
        compiler_params=PARAMS,
        cost_estimate=estimate(0, 6 * weights[0].shape[0] * units),
        name="load",
    )(*in_hbm(weights))


def sums_kernel(following, tok, grad, gate_b, up_b, down_b, *refs):
    copies = []
    if following is not None:
        hbm, out, kept, sems = refs[:3], refs[3], refs[4:7], refs[7]
        copies = fetches(following, hbm, kept, sems)
    else:
        (out,) = refs
    for copy in copies:
        copy.start()

    @pl.when(lax.axis_index("col") >= 0)
    def _():
        out[0] = dot(tok[...], gate_b[...]).astype(out.dtype)
        out[1] = dot(tok[...], up_b[...]).astype(out.dtype)
        out[2] = back_dot(grad[...], down_b[...]).astype(out.dtype)

    for copy in copies:
        copy.wait()


def partial_sums(block, tok, grad, dtype, weights=None, following=None):
    total, width = tok.shape
    units = block[2].shape[0]
    more = following is not None
    shapes = block_shapes(units, width) if more else []
    return pl.pallas_call(
        functools.partial(sums_kernel, following),
        in_specs=[WHOLE] * 5 + [HOLD] * (3 * more),
        out_specs=[WHOLE] * (1 + 3 * more),
        scratch_shapes=[pltpu.SemaphoreType.DMA((FETCHES, 3))] * more,
        out_shape=[array((3, total, units), dtype)] + [vmem_array(x) for x in shapes],
        compiler_params=PARAMS,
        cost_estimate=estimate(6 * total * width * units, 6 * width * units),
        name="partial_sums",
    )(tok, grad, *in_vmem(block), *(in_hbm(weights) if more else ()))


def combine_kernel(own, other, out):
    out[...] = (own[...] + other[...].astype(F32)).astype(BF16)


def combine(own, other):
    return pl.pallas_call(
        combine_kernel,
        out_shape=array(own.shape, BF16),
        compiler_params=PARAMS,
        cost_estimate=estimate(own.size, 8 * own.size),
        name="combine",
    )(own, other)


def activate_kernel(own, *refs):
    others, out = refs[:-1], refs[-1]
    gate, up, hidden_grad = (
        functools.reduce(lambda s, o: s + o[j].astype(F32), others, own[j]) for j in range(3)
    )
    sig = jax.nn.sigmoid(gate)
    swish = gate * sig
    out[0] = (swish * up).astype(BF16)
    out[1] = (hidden_grad * up * sig * (1.0 + gate * (1.0 - sig))).astype(BF16)
    out[2] = (hidden_grad * swish).astype(BF16)


def activate(own, others):
    return pl.pallas_call(
        activate_kernel,
        out_shape=array(own.shape, BF16),
        compiler_params=PARAMS,
        cost_estimate=estimate(8 * own.size, 12 * own.size),
        name="activate",
    )(own, *others)


def use_kernel(k, first, last, with_products, with_grads, act, *refs):
    refs = list(refs)
    leaving = []
    if with_products:
        gate_w, up_w, down_w = (refs.pop(0) for _ in range(3))
        before = None if first else refs.pop(0)
    if with_grads:
        tok_t, grad = refs.pop(0), refs.pop(0)
        gate_s, up_s, down_s, sems = refs[-4:]
        refs = refs[:-4]
        gate_g, up_g, down_g = refs[-3:]
        refs = refs[:-3]
        units, width = down_s.shape
        part, rows = width // CHUNKS, units // CHUNKS
        hidden_t = act[0].astype(F32).T.astype(BF16)
        mine = unit_block(k, units)
        start = jnp.bitwise_xor(lax.axis_index("col"), k) * units
        for i in range(CHUNKS):
            here, some = span(i, part), span(i, rows)
            gate_s[here] = dot(tok_t[here], act[1]).astype(BF16)
            up_s[here] = dot(tok_t[here], act[2]).astype(BF16)
            down_s[some] = dot(hidden_t[some], grad[...]).astype(BF16)
            there = pl.ds(i * part, part)
            below = pl.ds(pl.multiple_of(start + i * rows, rows), rows)
            ends = (
                (gate_s.at[there], gate_g.at[there, mine]),
                (up_s.at[there], up_g.at[there, mine]),
                (down_s.at[pl.ds(i * rows, rows)], down_g.at[below]),
            )
            for j, (source, target) in enumerate(ends):
                copy = pltpu.make_async_copy(source, target, sems.at[i, j])
                copy.start()
                leaving.append(copy)
    if with_products:
        outs = refs[-1 - last :]
        for i in range(down_w.shape[1] // PIECE):
            here = span(i, PIECE)
            back = back_dot(act[1], gate_w[here]) + back_dot(act[2], up_w[here])
            for j, term in enumerate((dot(act[0], down_w[:, here]), back)):
                term = term if first else before[j, :, here] + term
                if last:
                    half = term.shape[0] // 2
                    outs[0][j, :, here] = term[:half]
                    outs[1][j, :, here] = term[half:]
                else:
                    outs[0][j, :, here] = term
    for copy in leaving:
        copy.wait()


def use(k, act, weights=None, terms=None, last=False, sides=None, grads=(), after=()):
    _, total, units = act.shape
    first = terms is None
    specs, args = [WHOLE], [act]
    out_specs, out_shape, scratch, aliases = [], [], [], {}
    moved = 0
    if weights is not None:
        width = weights[2].shape[1]
        specs += [WHOLE] * 3
        args += in_vmem(weights)
        if not first:
            specs.append(WHOLE)
            args.append(terms)
        held = total // 2 if last else total
        out_specs += [WHOLE] * (1 + last)
        out_shape += [array((2, held, width), F32)] * (1 + last)
        moved += 6 * width * units
    if sides is not None:
        tok_t, grad, all_units = sides
        width = grad.shape[1]
        specs += [WHOLE, WHOLE]
        args += [tok_t, grad]
        for j, grad_before in enumerate(grads):
            aliases[len(args)] = len(out_shape) + j
            specs.append(HOLD)
            args.append(grad_before)
        out_specs += [HOLD] * 3
        out_shape += [pltpu.HBM((width, all_units), BF16)] * 2
        out_shape.append(pltpu.HBM((all_units, width), BF16))
        scratch += [pltpu.VMEM((width, units), BF16)] * 2
        scratch += [pltpu.VMEM((units, width), BF16), pltpu.SemaphoreType.DMA((CHUNKS, 3))]
        moved += 6 * width * units
    return pl.pallas_call(
        functools.partial(use_kernel, k, first, last, weights is not None, sides is not None),
        in_specs=specs + [HOLD] * len(after),
        out_specs=out_specs,
        scratch_shapes=scratch,
        out_shape=out_shape,
        input_output_aliases=aliases,
        compiler_params=PARAMS,
        cost_estimate=estimate(total * moved, moved),
        name=("products" if weights else "") + ("grads" if sides else ""),
    )(*args, *after)


def fold_kernel(rows, own, other, keep, *sent):
    total = own[...] + other[...]
    keep[...] = total[:, :rows]
    for i, out in enumerate(sent, 1):
        out[...] = total[:, i * rows : (i + 1) * rows].astype(BF16)


def fold(own, other, rows):
    _, total, width = own.shape
    others = total // rows - 1
    return pl.pallas_call(
        functools.partial(fold_kernel, rows),
        out_shape=[array((2, rows, width), F32)] + [array((2, rows, width), BF16)] * others,
        compiler_params=PARAMS,
        cost_estimate=estimate(own.size, 12 * own.size),
        name="fold",
    )(own, other)


def finish_kernel(own, *refs):
    others, outs = refs[:-2], refs[-2:]
    for j, out in enumerate(outs):
        total = functools.reduce(lambda s, o: s + o[j].astype(F32), others, own[j])
        out[...] = total.astype(BF16)


def finish(own, others):
    return pl.pallas_call(
        finish_kernel,
        out_shape=[array(own.shape[1:], BF16)] * 2,
        compiler_params=PARAMS,
        cost_estimate=estimate(own.size, 12 * own.size),
        name="finish",
    )(own, *others)


def pairwise(n_row, n_col, tokens, gate_weight, up_weight, down_weight, out_grad):
    rows = tokens.shape[0]
    all_units = gate_weight.shape[1]
    units = all_units // n_col
    weights = (gate_weight, up_weight, down_weight)
    along_row = functools.partial(swap, axis="row", size=n_row)
    along_col = functools.partial(swap, axis="col", size=n_col)

    mine = pack(tokens, out_grad)
    last_weights = load(3, weights, units)
    away = [along_row(mine, k=k) for k in range(2, n_row, 2)]
    away, last_weights = lax.optimization_barrier((away, last_weights))
    even = [mine, *away]
    odd = [along_row(piece, k=1) for piece in even]
    tok, grad, tok_t = assemble(even + odd, rows)
    sides = (tok_t, grad, all_units)

    there, *near_weights = partial_sums(last_weights, tok, grad, BF16, weights, 1)
    near = along_col(there, k=1)
    there, *far_weights = partial_sums(near_weights, tok, grad, BF16, weights, 2)
    from_near = along_col(there, k=1)
    here, *own_weights = partial_sums(far_weights, tok, grad, F32, weights, 0)
    from_far = along_col(combine(here, near), k=2)
    (here,) = partial_sums(own_weights, tok, grad, F32)
    own = activate(here, [from_near, from_far])

    near_act = along_col(own, k=1)
    far_act = along_col(own, k=2)
    terms, *grads = use(0, own, own_weights, sides=sides)
    terms, *grads = use(1, near_act, near_weights, terms, sides=sides, grads=grads)
    held, _ = lax.optimization_barrier((far_act, (terms, grads)))
    last_act = along_col(held, k=1)
    terms, *grads = use(2, far_act, far_weights, terms, sides=sides, grads=grads)
    kept, given = use(3, last_act, last_weights, terms, last=True)

    other = along_row(given, k=1)
    mine, *sent = fold(kept, other, rows)
    parts = [along_row(piece, k=2 * i) for i, piece in enumerate(sent, 1)]
    grads = use(3, last_act, sides=sides, grads=grads, after=(mine,))
    mixed, input_grad = finish(mine, parts)
    return (mixed, input_grad, *grads)


def gathered(tokens, gate_weight, up_weight, down_weight, out_grad):
    tok = lax.all_gather(tokens, "row", axis=0, tiled=True)
    grad = lax.all_gather(out_grad, "row", axis=0, tiled=True)

    def total(x):
        return lax.psum_scatter(x, "col", scatter_dimension=0, tiled=True)

    def outer(a, b):
        return lax.dot_general(a, b, CONTRACT, preferred_element_type=F32).astype(BF16)

    gate, up = total(dot(tok, gate_weight)), total(dot(tok, up_weight))
    hidden_grad = total(back_dot(grad, down_weight))
    sig = jax.nn.sigmoid(gate)
    swish = gate * sig
    hidden = (swish * up).astype(BF16)
    gate_delta = (hidden_grad * up * sig * (1.0 + gate * (1.0 - sig))).astype(BF16)
    up_delta = (hidden_grad * swish).astype(BF16)
    hidden, gate_delta, up_delta = (
        lax.all_gather(x, "col", axis=0, tiled=True) for x in (hidden, gate_delta, up_delta)
    )
    mixed = dot(hidden, down_weight)
    input_grad = back_dot(gate_delta, gate_weight) + back_dot(up_delta, up_weight)
    mixed, input_grad = (
        lax.psum_scatter(x, "row", scatter_dimension=0, tiled=True).astype(BF16)
        for x in (mixed, input_grad)
    )
    return (
        mixed,
        input_grad,
        outer(tok, gate_delta),
        outer(tok, up_delta),
        outer(hidden, grad),
    )


def solution(mesh):
    n_row, n_col = mesh.shape["row"], mesh.shape["col"]

    def shards(*args):
        tokens, gate_weight = args[:2]
        fits = (
            n_row & (n_row - 1) == 0
            and n_row > 1
            and n_col == 4
            and tokens.shape[0] % 8 == 0
            and tokens.shape[1] % (128 * CHUNKS) == 0
            and gate_weight.shape[1] % (128 * n_col) == 0
            and gate_weight.shape[1] % (16 * CHUNKS * n_col) == 0
            and tokens.shape[1] % PIECE == 0
            and 6 * gate_weight.size <= 36 * 1024 * 1024
        )
        if fits:
            return pairwise(n_row, n_col, *args)
        return gathered(*args)

    return jax.shard_map(
        shards,
        mesh=mesh,
        in_specs=(
            P("row", "col"),
            P("col", "row"),
            P("col", "row"),
            P("row", "col"),
            P("row", "col"),
        ),
        out_specs=(
            P("row", "col"),
            P("row", "col"),
            P("col", "row"),
            P("col", "row"),
            P("row", "col"),
        ),
        check_vma=False,
    )
```

```python
import functools

import jax
import jax.numpy as jnp
from jax import lax
from jax.experimental import pallas as pl
from jax.experimental.pallas import tpu as pltpu
from jax.sharding import PartitionSpec as P

BF16 = jnp.bfloat16
F32 = jnp.float32
VMEM_LIMIT = 14 * 1024 * 1024
CHUNKS = 8
FETCHES = 4
BACK = (((1,), (1,)), ((), ()))
CONTRACT = (((0,), (0,)), ((), ()))
PARAMS = pltpu.CompilerParams(vmem_limit_bytes=VMEM_LIMIT)
HOLD = pl.BlockSpec(memory_space=pl.ANY)
PIECE = 512
WHOLE = pl.BlockSpec(memory_space=pltpu.VMEM)


def dot(a, b):
    return jnp.dot(a, b, preferred_element_type=F32)


def back_dot(a, b):
    return lax.dot_general(a, b, BACK, preferred_element_type=F32)


def swap(x, axis, size, k):
    return lax.ppermute(x, axis, [(i, i ^ k) for i in range(size)])


def estimate(flops, num_bytes):
    return pl.CostEstimate(flops=flops // 8, bytes_accessed=num_bytes // 8, transcendentals=0)


def vmem_array(shape):
    return pltpu.VMEM(shape, BF16)


def in_vmem(arrays):
    return [pltpu.with_memory_space_constraint(x, pltpu.VMEM) for x in arrays]


def in_hbm(arrays):
    return [pltpu.with_memory_space_constraint(x, pltpu.HBM) for x in arrays]


def array(shape, dtype):
    return jax.ShapeDtypeStruct(shape, dtype)


def pack_kernel(tokens, out_grad, out):
    joined = jnp.concatenate([tokens[...].astype(F32), out_grad[...].astype(F32)], axis=0)
    out[...] = joined.astype(BF16)


def pack(tokens, out_grad):
    rows, width = tokens.shape
    return pl.pallas_call(
        pack_kernel,
        out_shape=array((2 * rows, width), BF16),
        compiler_params=PARAMS,
        cost_estimate=estimate(0, 8 * rows * width),
        name="pack",
    )(*in_hbm((tokens, out_grad)))


def assemble_kernel(rows, *refs):
    pieces, (tok, grad, tok_t) = refs[:-3], refs[-3:]
    both = [p[...].astype(F32) for p in pieces]
    all_tok = jnp.concatenate([b[:rows] for b in both], axis=0)
    all_grad = jnp.concatenate([b[rows:] for b in both], axis=0)
    tok[...] = all_tok.astype(BF16)
    grad[...] = all_grad.astype(BF16)
    tok_t[...] = all_tok.T.astype(BF16)


def assemble(pieces, rows):
    total, width = rows * len(pieces), pieces[0].shape[1]
    flat = (total, width)
    return pl.pallas_call(
        functools.partial(assemble_kernel, rows),
        out_shape=[array(shape, BF16) for shape in (flat, flat, (width, total))],
        compiler_params=PARAMS,
        cost_estimate=estimate(0, 12 * total * width),
        name="assemble",
    )(*pieces)


def unit_block(k, units):
    start = jnp.bitwise_xor(lax.axis_index("col"), k) * units
    return pl.ds(pl.multiple_of(start, units), units)


def span(i, size):
    return slice(i * size, (i + 1) * size)


def fetches(k, hbm, vmem, sems):
    units, width = vmem[2].shape
    mine = unit_block(k, units)
    start = jnp.bitwise_xor(lax.axis_index("col"), k) * units
    tall, wide = width // FETCHES, units // FETCHES
    copies = []
    for i in range(FETCHES):
        rows, some = pl.ds(i * tall, tall), pl.ds(i * wide, wide)
        below = pl.ds(pl.multiple_of(start + i * wide, wide), wide)
        ends = (
            (hbm[0].at[rows, mine], vmem[0].at[rows]),
            (hbm[1].at[rows, mine], vmem[1].at[rows]),
            (hbm[2].at[below], vmem[2].at[some]),
        )
        copies += [pltpu.make_async_copy(*ends[j], sems.at[i, j]) for j in range(3)]
    return copies


def block_shapes(units, width):
    return [(width, units), (width, units), (units, width)]


def load_kernel(k, *refs):
    copies = fetches(k, refs[:3], refs[-4:-1], refs[-1])
    for copy in copies:
        copy.start()
    for copy in copies:
        copy.wait()


def load(k, weights, units, after=()):
    shapes = block_shapes(units, weights[0].shape[0])
    return pl.pallas_call(
        functools.partial(load_kernel, k),
        in_specs=[HOLD] * (3 + len(after)),
        out_specs=[WHOLE] * 3,
        scratch_shapes=[pltpu.SemaphoreType.DMA((FETCHES, 3))],
        out_shape=[vmem_array(x) for x in shapes],
        compiler_params=PARAMS,
        cost_estimate=estimate(0, 6 * weights[0].shape[0] * units),
        name="load",
    )(*in_hbm(weights), *after)


def sums_kernel(following, tok, grad, gate_b, up_b, down_b, *refs):
    copies = []
    if following is not None:
        hbm, out, kept, sems = refs[:3], refs[3], refs[4:7], refs[7]
        copies = fetches(following, hbm, kept, sems)
    else:
        (out,) = refs
    for copy in copies:
        copy.start()

    @pl.when(lax.axis_index("col") >= 0)
    def _():
        out[0] = dot(tok[...], gate_b[...]).astype(out.dtype)
        out[1] = dot(tok[...], up_b[...]).astype(out.dtype)
        out[2] = back_dot(grad[...], down_b[...]).astype(out.dtype)

    for copy in copies:
        copy.wait()


def partial_sums(block, tok, grad, dtype, weights=None, following=None):
    total, width = tok.shape
    units = block[2].shape[0]
    more = following is not None
    shapes = block_shapes(units, width) if more else []
    return pl.pallas_call(
        functools.partial(sums_kernel, following),
        in_specs=[WHOLE] * 5 + [HOLD] * (3 * more),
        out_specs=[WHOLE] * (1 + 3 * more),
        scratch_shapes=[pltpu.SemaphoreType.DMA((FETCHES, 3))] * more,
        out_shape=[array((3, total, units), dtype)] + [vmem_array(x) for x in shapes],
        compiler_params=PARAMS,
        cost_estimate=estimate(6 * total * width * units, 6 * width * units),
        name="partial_sums",
    )(tok, grad, *in_vmem(block), *(in_hbm(weights) if more else ()))


def combine_kernel(own, other, out, token):
    token[...] = jnp.zeros_like(token)
    out[...] = (own[...] + other[...].astype(F32)).astype(BF16)


def combine(own, other):
    return pl.pallas_call(
        combine_kernel,
        out_shape=[array(own.shape, BF16), array((8, 128), F32)],
        compiler_params=PARAMS,
        cost_estimate=estimate(own.size, 8 * own.size),
        name="combine",
    )(own, other)


def activate_kernel(own, *refs):
    others, (out, hidden, deltas) = refs[:-3], refs[-3:]
    gate, up, hidden_grad = (
        functools.reduce(lambda s, o: s + o[j].astype(F32), others, own[j]) for j in range(3)
    )
    sig = jax.nn.sigmoid(gate)
    swish = gate * sig
    out[0] = (swish * up).astype(BF16)
    out[1] = (hidden_grad * up * sig * (1.0 + gate * (1.0 - sig))).astype(BF16)
    out[2] = (hidden_grad * swish).astype(BF16)
    hidden[...] = out[0]
    deltas[...] = out[1:]


def activate(own, others):
    return pl.pallas_call(
        activate_kernel,
        out_shape=[array(x, BF16) for x in (own.shape, own.shape[1:], (2, *own.shape[1:]))],
        compiler_params=PARAMS,
        cost_estimate=estimate(8 * own.size, 12 * own.size),
        name="activate",
    )(own, *others)


def use_kernel(k, first, last, with_products, with_grads, apart, *refs):
    refs = list(refs)
    if apart:
        hidden, deltas = refs.pop(0), refs.pop(0)
        act = hidden[...], deltas[0], deltas[1]
    else:
        whole = refs.pop(0)
        act = whole[0], whole[1], whole[2]
    leaving = []
    if with_products:
        gate_w, up_w, down_w = (refs.pop(0) for _ in range(3))
        before = None if first else refs.pop(0)
    if with_grads:
        tok_t, grad = refs.pop(0), refs.pop(0)
        gate_s, up_s, down_s, sems = refs[-4:]
        refs = refs[:-4]
        gate_g, up_g, down_g = refs[-3:]
        refs = refs[:-3]
        units, width = down_s.shape
        part, rows = width // CHUNKS, units // CHUNKS
        hidden_t = act[0].astype(F32).T.astype(BF16)
        mine = unit_block(k, units)
        start = jnp.bitwise_xor(lax.axis_index("col"), k) * units
        for i in range(CHUNKS):
            here, some = span(i, part), span(i, rows)
            gate_s[here] = dot(tok_t[here], act[1]).astype(BF16)
            up_s[here] = dot(tok_t[here], act[2]).astype(BF16)
            down_s[some] = dot(hidden_t[some], grad[...]).astype(BF16)
            there = pl.ds(i * part, part)
            below = pl.ds(pl.multiple_of(start + i * rows, rows), rows)
            ends = (
                (gate_s.at[there], gate_g.at[there, mine]),
                (up_s.at[there], up_g.at[there, mine]),
                (down_s.at[pl.ds(i * rows, rows)], down_g.at[below]),
            )
            for j, (source, target) in enumerate(ends):
                copy = pltpu.make_async_copy(source, target, sems.at[i, j])
                copy.start()
                leaving.append(copy)
    if with_products:
        outs = refs[-1 - last :]
        for i in range(down_w.shape[1] // PIECE):
            here = span(i, PIECE)
            back = back_dot(act[1], gate_w[here]) + back_dot(act[2], up_w[here])
            for j, term in enumerate((dot(act[0], down_w[:, here]), back)):
                term = term if first else before[j, :, here] + term
                if last:
                    half = term.shape[0] // 2
                    outs[0][j, :, here] = term[:half]
                    outs[1][j, :, here] = term[half:]
                else:
                    outs[0][j, :, here] = term
    for copy in leaving:
        copy.wait()


def use(k, act, weights=None, terms=None, last=False, sides=None, grads=(), after=()):
    total, units = act[-1].shape[1:]
    first = terms is None
    specs, args = [WHOLE] * len(act), list(act)
    out_specs, out_shape, scratch, aliases = [], [], [], {}
    moved = 0
    if weights is not None:
        width = weights[2].shape[1]
        specs += [WHOLE] * 3
        args += in_vmem(weights)
        if not first:
            specs.append(WHOLE)
            args.append(terms)
        held = total // 2 if last else total
        out_specs += [WHOLE] * (1 + last)
        out_shape += [array((2, held, width), F32)] * (1 + last)
        moved += 6 * width * units
    if sides is not None:
        tok_t, grad, all_units = sides
        width = grad.shape[1]
        specs += [WHOLE, WHOLE]
        args += [tok_t, grad]
        for j, grad_before in enumerate(grads):
            aliases[len(args)] = len(out_shape) + j
            specs.append(HOLD)
            args.append(grad_before)
        out_specs += [HOLD] * 3
        out_shape += [pltpu.HBM((width, all_units), BF16)] * 2
        out_shape.append(pltpu.HBM((all_units, width), BF16))
        scratch += [pltpu.VMEM((width, units), BF16)] * 2
        scratch += [pltpu.VMEM((units, width), BF16), pltpu.SemaphoreType.DMA((CHUNKS, 3))]
        moved += 6 * width * units
    return pl.pallas_call(
        functools.partial(
            use_kernel, k, first, last, weights is not None, sides is not None, len(act) == 2
        ),
        in_specs=specs + [HOLD] * len(after),
        out_specs=out_specs,
        scratch_shapes=scratch,
        out_shape=out_shape,
        input_output_aliases=aliases,
        compiler_params=PARAMS,
        cost_estimate=estimate(total * moved, moved),
        name=("products" if weights else "") + ("grads" if sides else ""),
    )(*args, *after)


def fold_kernel(rows, own, other, keep, *sent):
    total = own[...] + other[...]
    keep[...] = total[:, :rows]
    for i, out in enumerate(sent, 1):
        out[...] = total[:, i * rows : (i + 1) * rows].astype(BF16)


def fold(own, other, rows):
    _, total, width = own.shape
    others = total // rows - 1
    return pl.pallas_call(
        functools.partial(fold_kernel, rows),
        out_shape=[array((2, rows, width), F32)] + [array((2, rows, width), BF16)] * others,
        compiler_params=PARAMS,
        cost_estimate=estimate(own.size, 12 * own.size),
        name="fold",
    )(own, other)


def finish_kernel(own, *refs):
    others, outs = refs[:-2], refs[-2:]
    for j, out in enumerate(outs):
        total = functools.reduce(lambda s, o: s + o[j].astype(F32), others, own[j])
        out[...] = total.astype(BF16)


def finish(own, others):
    return pl.pallas_call(
        finish_kernel,
        out_shape=[array(own.shape[1:], BF16)] * 2,
        compiler_params=PARAMS,
        cost_estimate=estimate(own.size, 12 * own.size),
        name="finish",
    )(own, *others)


def pairwise(n_row, n_col, tokens, gate_weight, up_weight, down_weight, out_grad):
    rows = tokens.shape[0]
    all_units = gate_weight.shape[1]
    units = all_units // n_col
    weights = (gate_weight, up_weight, down_weight)
    along_row = functools.partial(swap, axis="row", size=n_row)
    along_col = functools.partial(swap, axis="col", size=n_col)

    mine = pack(tokens, out_grad)
    last_weights = load(3, weights, units)
    away = [along_row(mine, k=k) for k in range(2, n_row, 2)]
    away, last_weights = lax.optimization_barrier((away, last_weights))
    even = [mine, *away]
    odd = [along_row(piece, k=1) for piece in even]
    tok, grad, tok_t = assemble(even + odd, rows)
    sides = (tok_t, grad, all_units)

    there, *near_weights = partial_sums(last_weights, tok, grad, BF16, weights, 1)
    near = along_col(there, k=1)
    there, *far_weights = partial_sums(near_weights, tok, grad, BF16, weights, 2)
    from_near = along_col(there, k=1)
    (here,) = partial_sums(far_weights, tok, grad, F32)
    pair, token = combine(here, near)
    from_far = along_col(pair, k=2)
    own_weights = load(0, weights, units, after=(token,))
    (here,) = partial_sums(own_weights, tok, grad, F32)
    own, hidden, deltas = activate(here, [from_near, from_far])

    near_act = along_col(own, k=1)
    (terms,) = use(0, (own,), own_weights)
    (hidden, deltas, own), _ = lax.optimization_barrier(((hidden, deltas, own), terms))
    far_deltas = along_col(deltas, k=2)
    far_hidden = along_col(hidden, k=2)
    grads = use(0, (own,), sides=sides)
    terms, *grads = use(1, (near_act,), near_weights, terms, sides=sides, grads=grads)
    far_deltas, _ = lax.optimization_barrier((far_deltas, (terms, grads)))
    last_deltas = along_col(far_deltas, k=1)
    far_hidden, _ = lax.optimization_barrier((far_hidden, (terms, grads)))
    last_hidden = along_col(far_hidden, k=1)
    far_act, last_act = (far_hidden, far_deltas), (last_hidden, last_deltas)
    terms, *grads = use(2, far_act, far_weights, terms, sides=sides, grads=grads)
    kept, given = use(3, last_act, last_weights, terms, last=True)

    other = along_row(given, k=1)
    mine, *sent = fold(kept, other, rows)
    parts = [along_row(piece, k=2 * i) for i, piece in enumerate(sent, 1)]
    grads = use(3, last_act, sides=sides, grads=grads, after=(mine,))
    mixed, input_grad = finish(mine, parts)
    return (mixed, input_grad, *grads)


def gathered(tokens, gate_weight, up_weight, down_weight, out_grad):
    tok = lax.all_gather(tokens, "row", axis=0, tiled=True)
    grad = lax.all_gather(out_grad, "row", axis=0, tiled=True)

    def total(x):
        return lax.psum_scatter(x, "col", scatter_dimension=0, tiled=True)

    def outer(a, b):
        return lax.dot_general(a, b, CONTRACT, preferred_element_type=F32).astype(BF16)

    gate, up = total(dot(tok, gate_weight)), total(dot(tok, up_weight))
    hidden_grad = total(back_dot(grad, down_weight))
    sig = jax.nn.sigmoid(gate)
    swish = gate * sig
    hidden = (swish * up).astype(BF16)
    gate_delta = (hidden_grad * up * sig * (1.0 + gate * (1.0 - sig))).astype(BF16)
    up_delta = (hidden_grad * swish).astype(BF16)
    hidden, gate_delta, up_delta = (
        lax.all_gather(x, "col", axis=0, tiled=True) for x in (hidden, gate_delta, up_delta)
    )
    mixed = dot(hidden, down_weight)
    input_grad = back_dot(gate_delta, gate_weight) + back_dot(up_delta, up_weight)
    mixed, input_grad = (
        lax.psum_scatter(x, "row", scatter_dimension=0, tiled=True).astype(BF16)
        for x in (mixed, input_grad)
    )
    return (
        mixed,
        input_grad,
        outer(tok, gate_delta),
        outer(tok, up_delta),
        outer(hidden, grad),
    )


def solution(mesh):
    n_row, n_col = mesh.shape["row"], mesh.shape["col"]

    def shards(*args):
        tokens, gate_weight = args[:2]
        fits = (
            n_row & (n_row - 1) == 0
            and n_row > 1
            and n_col == 4
            and tokens.shape[0] % 8 == 0
            and tokens.shape[1] % (128 * CHUNKS) == 0
            and gate_weight.shape[1] % (128 * n_col) == 0
            and gate_weight.shape[1] % (16 * CHUNKS * n_col) == 0
            and tokens.shape[1] % PIECE == 0
            and 6 * gate_weight.size <= 36 * 1024 * 1024
        )
        if fits:
            return pairwise(n_row, n_col, *args)
        return gathered(*args)

    return jax.shard_map(
        shards,
        mesh=mesh,
        in_specs=(
            P("row", "col"),
            P("col", "row"),
            P("col", "row"),
            P("row", "col"),
            P("row", "col"),
        ),
        out_specs=(
            P("row", "col"),
            P("row", "col"),
            P("col", "row"),
            P("col", "row"),
            P("row", "col"),
        ),
        check_vma=False,
    )
```

```python
import functools

import jax
import jax.numpy as jnp
from jax import lax
from jax.experimental import pallas as pl
from jax.experimental.pallas import tpu as pltpu
from jax.sharding import PartitionSpec as P

BF16 = jnp.bfloat16
F32 = jnp.float32
VMEM_LIMIT = 14 * 1024 * 1024
CHUNKS = 8
FETCHES = 4
BACK = (((1,), (1,)), ((), ()))
CONTRACT = (((0,), (0,)), ((), ()))
PARAMS = pltpu.CompilerParams(vmem_limit_bytes=VMEM_LIMIT)
HOLD = pl.BlockSpec(memory_space=pl.ANY)
PIECE = 512
WHOLE = pl.BlockSpec(memory_space=pltpu.VMEM)


def dot(a, b):
    return jnp.dot(a, b, preferred_element_type=F32)


def back_dot(a, b):
    return lax.dot_general(a, b, BACK, preferred_element_type=F32)


def swap(x, axis, size, k):
    return lax.ppermute(x, axis, [(i, i ^ k) for i in range(size)])


def estimate(flops, num_bytes):
    return pl.CostEstimate(flops=flops // 8, bytes_accessed=num_bytes // 8, transcendentals=0)


def vmem_array(shape):
    return pltpu.VMEM(shape, BF16)


def in_vmem(arrays):
    return [pltpu.with_memory_space_constraint(x, pltpu.VMEM) for x in arrays]


def in_hbm(arrays):
    return [pltpu.with_memory_space_constraint(x, pltpu.HBM) for x in arrays]


def array(shape, dtype):
    return jax.ShapeDtypeStruct(shape, dtype)


def pack_kernel(tokens, out_grad, out):
    joined = jnp.concatenate([tokens[...].astype(F32), out_grad[...].astype(F32)], axis=0)
    out[...] = joined.astype(BF16)


def pack(tokens, out_grad):
    rows, width = tokens.shape
    return pl.pallas_call(
        pack_kernel,
        out_shape=array((2 * rows, width), BF16),
        compiler_params=PARAMS,
        cost_estimate=estimate(0, 8 * rows * width),
        name="pack",
    )(*in_hbm((tokens, out_grad)))


def assemble_kernel(rows, *refs):
    pieces, (tok, grad, tok_t) = refs[:-3], refs[-3:]
    both = [p[...].astype(F32) for p in pieces]
    all_tok = jnp.concatenate([b[:rows] for b in both], axis=0)
    all_grad = jnp.concatenate([b[rows:] for b in both], axis=0)
    tok[...] = all_tok.astype(BF16)
    grad[...] = all_grad.astype(BF16)
    tok_t[...] = all_tok.T.astype(BF16)


def assemble(pieces, rows):
    total, width = rows * len(pieces), pieces[0].shape[1]
    flat = (total, width)
    return pl.pallas_call(
        functools.partial(assemble_kernel, rows),
        out_shape=[array(shape, BF16) for shape in (flat, flat, (width, total))],
        compiler_params=PARAMS,
        cost_estimate=estimate(0, 12 * total * width),
        name="assemble",
    )(*pieces)


def unit_block(k, units):
    start = jnp.bitwise_xor(lax.axis_index("col"), k) * units
    return pl.ds(pl.multiple_of(start, units), units)


def span(i, size):
    return slice(i * size, (i + 1) * size)


def fetches(k, hbm, vmem, sems):
    units, width = vmem[2].shape
    mine = unit_block(k, units)
    start = jnp.bitwise_xor(lax.axis_index("col"), k) * units
    tall, wide = width // FETCHES, units // FETCHES
    copies = []
    for i in range(FETCHES):
        rows, some = pl.ds(i * tall, tall), pl.ds(i * wide, wide)
        below = pl.ds(pl.multiple_of(start + i * wide, wide), wide)
        ends = (
            (hbm[0].at[rows, mine], vmem[0].at[rows]),
            (hbm[1].at[rows, mine], vmem[1].at[rows]),
            (hbm[2].at[below], vmem[2].at[some]),
        )
        copies += [pltpu.make_async_copy(*ends[j], sems.at[i, j]) for j in range(3)]
    return copies


def block_shapes(units, width):
    return [(width, units), (width, units), (units, width)]


def load_kernel(k, *refs):
    copies = fetches(k, refs[:3], refs[-4:-1], refs[-1])
    for copy in copies:
        copy.start()
    for copy in copies:
        copy.wait()


def load(k, weights, units, after=()):
    shapes = block_shapes(units, weights[0].shape[0])
    return pl.pallas_call(
        functools.partial(load_kernel, k),
        in_specs=[HOLD] * (3 + len(after)),
        out_specs=[WHOLE] * 3,
        scratch_shapes=[pltpu.SemaphoreType.DMA((FETCHES, 3))],
        out_shape=[vmem_array(x) for x in shapes],
        compiler_params=PARAMS,
        cost_estimate=estimate(0, 6 * weights[0].shape[0] * units),
        name="load",
    )(*in_hbm(weights), *after)


def sums_kernel(following, apart, after, tok, grad, gate_b, up_b, down_b, *refs):
    copies = []
    if following is not None:
        hbm, refs = refs[:3], refs[3:]
    refs = refs[after:]
    if apart:
        out, back = refs[:2]
    else:
        out, back = refs[0], refs[0].at[2]
    if following is not None:
        copies = fetches(following, hbm, refs[1 + apart : 4 + apart], refs[4 + apart])
    for copy in copies:
        copy.start()

    @pl.when(lax.axis_index("col") >= 0)
    def _():
        out[0] = dot(tok[...], gate_b[...]).astype(out.dtype)
        out[1] = dot(tok[...], up_b[...]).astype(out.dtype)
        back[...] = back_dot(grad[...], down_b[...]).astype(out.dtype)

    for copy in copies:
        copy.wait()


def partial_sums(
    block, tok, grad, dtype, weights=None, following=None, apart=False, after=()
):
    total, width = tok.shape
    units = block[2].shape[0]
    more = following is not None
    shapes = block_shapes(units, width) if more else []
    sums = [(2, total, units), (total, units)] if apart else [(3, total, units)]
    return pl.pallas_call(
        functools.partial(sums_kernel, following, apart, len(after)),
        in_specs=[WHOLE] * 5 + [HOLD] * (3 * more + len(after)),
        out_specs=[WHOLE] * (len(sums) + 3 * more),
        scratch_shapes=[pltpu.SemaphoreType.DMA((FETCHES, 3))] * more,
        out_shape=[array(x, dtype) for x in sums] + [vmem_array(x) for x in shapes],
        compiler_params=PARAMS,
        cost_estimate=estimate(6 * total * width * units, 6 * width * units),
        name="partial_sums",
    )(tok, grad, *in_vmem(block), *(in_hbm(weights) if more else ()), *after)


def combine_kernel(own, other, *refs):
    out, token = refs[-2:]
    token[...] = jnp.zeros_like(token)
    out[...] = (own[...] + other[...].astype(F32)).astype(BF16)


def combine(own, other, after=()):
    return pl.pallas_call(
        combine_kernel,
        in_specs=[WHOLE, WHOLE] + [HOLD] * len(after),
        out_shape=[array(own.shape, BF16), array((8, 128), F32)],
        compiler_params=PARAMS,
        cost_estimate=estimate(own.size, 8 * own.size),
        name="combine",
    )(own, other, *after)


def activate_kernel(own, near, far, far_back, out, hidden, deltas):
    gate, up = (own[j] + near[j].astype(F32) + far[j].astype(F32) for j in range(2))
    hidden_grad = own[2] + near[2].astype(F32) + far_back[...].astype(F32)
    sig = jax.nn.sigmoid(gate)
    swish = gate * sig
    out[0] = (swish * up).astype(BF16)
    out[1] = (hidden_grad * up * sig * (1.0 + gate * (1.0 - sig))).astype(BF16)
    out[2] = (hidden_grad * swish).astype(BF16)
    hidden[...] = out[0]
    deltas[...] = out[1:]


def activate(own, others):
    return pl.pallas_call(
        activate_kernel,
        out_shape=[array(x, BF16) for x in (own.shape, own.shape[1:], (2, *own.shape[1:]))],
        compiler_params=PARAMS,
        cost_estimate=estimate(8 * own.size, 12 * own.size),
        name="activate",
    )(own, *others)


def use_kernel(k, first, last, with_products, with_grads, apart, *refs):
    refs = list(refs)
    if apart:
        hidden, deltas = refs.pop(0), refs.pop(0)
        act = hidden, deltas.at[0], deltas.at[1]
    else:
        whole = refs.pop(0)
        act = whole.at[0], whole.at[1], whole.at[2]
    leaving = []
    if with_products:
        gate_w, up_w, down_w = (refs.pop(0) for _ in range(3))
        before = None if first else refs.pop(0)
    if with_grads:
        tok_t, grad = refs.pop(0), refs.pop(0)
        gate_s, up_s, down_s, sems = refs[-4:]
        refs = refs[:-4]
        gate_g, up_g, down_g = refs[-3:]
        refs = refs[:-3]
        units, width = down_s.shape
        part, rows = width // CHUNKS, units // CHUNKS
        hidden_t = act[0][...].astype(F32).T.astype(BF16)
        mine = unit_block(k, units)
        start = jnp.bitwise_xor(lax.axis_index("col"), k) * units
        for i in range(CHUNKS):
            here, some = span(i, part), span(i, rows)
            gate_s[here] = dot(tok_t[here], act[1][...]).astype(BF16)
            up_s[here] = dot(tok_t[here], act[2][...]).astype(BF16)
            down_s[some] = dot(hidden_t[some], grad[...]).astype(BF16)
            there = pl.ds(i * part, part)
            below = pl.ds(pl.multiple_of(start + i * rows, rows), rows)
            ends = (
                (gate_s.at[there], gate_g.at[there, mine]),
                (up_s.at[there], up_g.at[there, mine]),
                (down_s.at[pl.ds(i * rows, rows)], down_g.at[below]),
            )
            for j, (source, target) in enumerate(ends):
                copy = pltpu.make_async_copy(source, target, sems.at[i, j])
                copy.start()
                leaving.append(copy)
    if with_products:
        outs = refs[-1 - last :]
        for i in range(down_w.shape[1] // PIECE):
            here = span(i, PIECE)
            back = back_dot(act[1][...], gate_w[here]) + back_dot(act[2][...], up_w[here])
            for j, term in enumerate((dot(act[0][...], down_w[:, here]), back)):
                term = term if first else before[j, :, here] + term
                if last:
                    half = term.shape[0] // 2
                    outs[0][j, :, here] = term[:half]
                    outs[1][j, :, here] = term[half:]
                else:
                    outs[0][j, :, here] = term
    for copy in leaving:
        copy.wait()


def use(k, act, weights=None, terms=None, last=False, sides=None, grads=(), after=()):
    total, units = act[-1].shape[1:]
    first = terms is None
    specs, args = [WHOLE] * len(act), list(act)
    out_specs, out_shape, scratch, aliases = [], [], [], {}
    moved = 0
    if weights is not None:
        width = weights[2].shape[1]
        specs += [WHOLE] * 3
        args += in_vmem(weights)
        if not first:
            specs.append(WHOLE)
            args.append(terms)
        held = total // 2 if last else total
        out_specs += [WHOLE] * (1 + last)
        out_shape += [array((2, held, width), F32)] * (1 + last)
        moved += 6 * width * units
    if sides is not None:
        tok_t, grad, all_units = sides
        width = grad.shape[1]
        specs += [WHOLE, WHOLE]
        args += [tok_t, grad]
        for j, grad_before in enumerate(grads):
            aliases[len(args)] = len(out_shape) + j
            specs.append(HOLD)
            args.append(grad_before)
        out_specs += [HOLD] * 3
        out_shape += [pltpu.HBM((width, all_units), BF16)] * 2
        out_shape.append(pltpu.HBM((all_units, width), BF16))
        scratch += [pltpu.VMEM((width, units), BF16)] * 2
        scratch += [pltpu.VMEM((units, width), BF16), pltpu.SemaphoreType.DMA((CHUNKS, 3))]
        moved += 6 * width * units
    return pl.pallas_call(
        functools.partial(
            use_kernel, k, first, last, weights is not None, sides is not None, len(act) == 2
        ),
        in_specs=specs + [HOLD] * len(after),
        out_specs=out_specs,
        scratch_shapes=scratch,
        out_shape=out_shape,
        input_output_aliases=aliases,
        compiler_params=PARAMS,
        cost_estimate=estimate(total * moved, moved),
        name=("products" if weights else "") + ("grads" if sides else ""),
    )(*args, *after)


def fold_kernel(rows, own, other, keep, *sent):
    total = own[...] + other[...]
    keep[...] = total[:, :rows]
    for i, out in enumerate(sent, 1):
        out[...] = total[:, i * rows : (i + 1) * rows].astype(BF16)


def fold(own, other, rows):
    _, total, width = own.shape
    others = total // rows - 1
    return pl.pallas_call(
        functools.partial(fold_kernel, rows),
        out_shape=[array((2, rows, width), F32)] + [array((2, rows, width), BF16)] * others,
        compiler_params=PARAMS,
        cost_estimate=estimate(own.size, 12 * own.size),
        name="fold",
    )(own, other)


def finish_kernel(own, *refs):
    others, outs = refs[:-2], refs[-2:]
    for j, out in enumerate(outs):
        total = functools.reduce(lambda s, o: s + o[j].astype(F32), others, own[j])
        out[...] = total.astype(BF16)


def finish(own, others):
    return pl.pallas_call(
        finish_kernel,
        out_shape=[array(own.shape[1:], BF16)] * 2,
        compiler_params=PARAMS,
        cost_estimate=estimate(own.size, 12 * own.size),
        name="finish",
    )(own, *others)


def pairwise(n_row, n_col, tokens, gate_weight, up_weight, down_weight, out_grad):
    rows = tokens.shape[0]
    all_units = gate_weight.shape[1]
    units = all_units // n_col
    weights = (gate_weight, up_weight, down_weight)
    along_row = functools.partial(swap, axis="row", size=n_row)
    along_col = functools.partial(swap, axis="col", size=n_col)

    mine = pack(tokens, out_grad)
    last_weights = load(3, weights, units)
    away = [along_row(mine, k=k) for k in range(2, n_row, 2)]
    away, last_weights = lax.optimization_barrier((away, last_weights))
    even = [mine, *away]
    odd = [along_row(piece, k=1) for piece in even]
    tok, grad, tok_t = assemble(even + odd, rows)
    sides = (tok_t, grad, all_units)

    sums = functools.partial(partial_sums, tok=tok, grad=grad)
    there, back, *far_weights = sums(
        last_weights, dtype=BF16, weights=weights, following=2, apart=True
    )
    near_back, near = along_col(back, k=1), along_col(there, k=1)
    here, back, *near_weights = sums(
        far_weights, dtype=F32, weights=weights, following=1, apart=True
    )
    pair_back, token = combine(back, near_back)
    far_back = along_col(pair_back, k=2)
    (there,) = sums(near_weights, dtype=BF16, after=(token,))
    from_near = along_col(there, k=1)
    pair, token = combine(here, near, after=(there, far_back))
    from_far = along_col(pair, k=2)
    own_weights = load(0, weights, units, after=(token,))
    (here,) = sums(own_weights, dtype=F32)
    own, hidden, deltas = activate(here, [from_near, from_far, far_back])

    near_act = along_col(own, k=1)
    (terms,) = use(0, (own,), own_weights)
    (hidden, deltas, own), _ = lax.optimization_barrier(((hidden, deltas, own), terms))
    far_deltas = along_col(deltas, k=2)
    far_hidden = along_col(hidden, k=2)
    grads = use(0, (own,), sides=sides)
    terms, *grads = use(1, (near_act,), near_weights, terms, sides=sides, grads=grads)
    far_deltas, _ = lax.optimization_barrier((far_deltas, (terms, grads)))
    last_deltas = along_col(far_deltas, k=1)
    far_hidden, _ = lax.optimization_barrier((far_hidden, (terms, grads)))
    last_hidden = along_col(far_hidden, k=1)
    far_act, last_act = (far_hidden, far_deltas), (last_hidden, last_deltas)
    terms, *grads = use(2, far_act, far_weights, terms, sides=sides, grads=grads)
    kept, given = use(3, last_act, last_weights, terms, last=True)

    other = along_row(given, k=1)
    mine, *sent = fold(kept, other, rows)
    parts = [along_row(piece, k=2 * i) for i, piece in enumerate(sent, 1)]
    grads = use(3, last_act, sides=sides, grads=grads, after=(mine,))
    mixed, input_grad = finish(mine, parts)
    return (mixed, input_grad, *grads)


def gathered(tokens, gate_weight, up_weight, down_weight, out_grad):
    tok = lax.all_gather(tokens, "row", axis=0, tiled=True)
    grad = lax.all_gather(out_grad, "row", axis=0, tiled=True)

    def total(x):
        return lax.psum_scatter(x, "col", scatter_dimension=0, tiled=True)

    def outer(a, b):
        return lax.dot_general(a, b, CONTRACT, preferred_element_type=F32).astype(BF16)

    gate, up = total(dot(tok, gate_weight)), total(dot(tok, up_weight))
    hidden_grad = total(back_dot(grad, down_weight))
    sig = jax.nn.sigmoid(gate)
    swish = gate * sig
    hidden = (swish * up).astype(BF16)
    gate_delta = (hidden_grad * up * sig * (1.0 + gate * (1.0 - sig))).astype(BF16)
    up_delta = (hidden_grad * swish).astype(BF16)
    hidden, gate_delta, up_delta = (
        lax.all_gather(x, "col", axis=0, tiled=True) for x in (hidden, gate_delta, up_delta)
    )
    mixed = dot(hidden, down_weight)
    input_grad = back_dot(gate_delta, gate_weight) + back_dot(up_delta, up_weight)
    mixed, input_grad = (
        lax.psum_scatter(x, "row", scatter_dimension=0, tiled=True).astype(BF16)
        for x in (mixed, input_grad)
    )
    return (
        mixed,
        input_grad,
        outer(tok, gate_delta),
        outer(tok, up_delta),
        outer(hidden, grad),
    )


def solution(mesh):
    n_row, n_col = mesh.shape["row"], mesh.shape["col"]

    def shards(*args):
        tokens, gate_weight = args[:2]
        fits = (
            n_row & (n_row - 1) == 0
            and n_row > 1
            and n_col == 4
            and tokens.shape[0] % 8 == 0
            and tokens.shape[1] % (128 * CHUNKS) == 0
            and gate_weight.shape[1] % (128 * n_col) == 0
            and gate_weight.shape[1] % (16 * CHUNKS * n_col) == 0
            and tokens.shape[1] % PIECE == 0
            and 6 * gate_weight.size <= 36 * 1024 * 1024
        )
        if fits:
            return pairwise(n_row, n_col, *args)
        return gathered(*args)

    return jax.shard_map(
        shards,
        mesh=mesh,
        in_specs=(
            P("row", "col"),
            P("col", "row"),
            P("col", "row"),
            P("row", "col"),
            P("row", "col"),
        ),
        out_specs=(
            P("row", "col"),
            P("row", "col"),
            P("col", "row"),
            P("col", "row"),
            P("row", "col"),
        ),
        check_vma=False,
    )
```

```python
import functools

import jax
import jax.numpy as jnp
from jax import lax
from jax.experimental import pallas as pl
from jax.experimental.pallas import tpu as pltpu
from jax.sharding import PartitionSpec as P

BF16 = jnp.bfloat16
F32 = jnp.float32
VMEM_LIMIT = 14 * 1024 * 1024
CHUNKS = 8
FETCHES = 4
BACK = (((1,), (1,)), ((), ()))
CONTRACT = (((0,), (0,)), ((), ()))
PARAMS = pltpu.CompilerParams(vmem_limit_bytes=VMEM_LIMIT)
HOLD = pl.BlockSpec(memory_space=pl.ANY)
PIECE = 512
WHOLE = pl.BlockSpec(memory_space=pltpu.VMEM)


def dot(a, b):
    return jnp.dot(a, b, preferred_element_type=F32)


def back_dot(a, b):
    return lax.dot_general(a, b, BACK, preferred_element_type=F32)


def swap(x, axis, size, k):
    return lax.ppermute(x, axis, [(i, i ^ k) for i in range(size)])


def estimate(flops, num_bytes):
    return pl.CostEstimate(flops=flops // 8, bytes_accessed=num_bytes // 8, transcendentals=0)


def vmem_array(shape):
    return pltpu.VMEM(shape, BF16)


def in_vmem(arrays):
    return [pltpu.with_memory_space_constraint(x, pltpu.VMEM) for x in arrays]


def in_hbm(arrays):
    return [pltpu.with_memory_space_constraint(x, pltpu.HBM) for x in arrays]


def array(shape, dtype):
    return jax.ShapeDtypeStruct(shape, dtype)


def pack_kernel(tokens, out_grad, out):
    joined = jnp.concatenate([tokens[...].astype(F32), out_grad[...].astype(F32)], axis=0)
    out[...] = joined.astype(BF16)


def pack(tokens, out_grad):
    rows, width = tokens.shape
    return pl.pallas_call(
        pack_kernel,
        out_shape=array((2 * rows, width), BF16),
        compiler_params=PARAMS,
        cost_estimate=estimate(0, 8 * rows * width),
        name="pack",
    )(*in_hbm((tokens, out_grad)))


def assemble_kernel(rows, *refs):
    pieces, (tok, grad, tok_t) = refs[:-3], refs[-3:]
    both = [p[...].astype(F32) for p in pieces]
    all_tok = jnp.concatenate([b[:rows] for b in both], axis=0)
    all_grad = jnp.concatenate([b[rows:] for b in both], axis=0)
    tok[...] = all_tok.astype(BF16)
    grad[...] = all_grad.astype(BF16)
    tok_t[...] = all_tok.T.astype(BF16)


def assemble(pieces, rows):
    total, width = rows * len(pieces), pieces[0].shape[1]
    flat = (total, width)
    return pl.pallas_call(
        functools.partial(assemble_kernel, rows),
        out_shape=[array(shape, BF16) for shape in (flat, flat, (width, total))],
        compiler_params=PARAMS,
        cost_estimate=estimate(0, 12 * total * width),
        name="assemble",
    )(*pieces)


def unit_block(k, units):
    start = jnp.bitwise_xor(lax.axis_index("col"), k) * units
    return pl.ds(pl.multiple_of(start, units), units)


def span(i, size):
    return slice(i * size, (i + 1) * size)


def fetches(k, hbm, vmem, sems):
    units, width = vmem[2].shape
    mine = unit_block(k, units)
    start = jnp.bitwise_xor(lax.axis_index("col"), k) * units
    tall, wide = width // FETCHES, units // FETCHES
    copies = []
    for i in range(FETCHES):
        rows, some = pl.ds(i * tall, tall), pl.ds(i * wide, wide)
        below = pl.ds(pl.multiple_of(start + i * wide, wide), wide)
        ends = (
            (hbm[0].at[rows, mine], vmem[0].at[rows]),
            (hbm[1].at[rows, mine], vmem[1].at[rows]),
            (hbm[2].at[below], vmem[2].at[some]),
        )
        copies += [pltpu.make_async_copy(*ends[j], sems.at[i, j]) for j in range(3)]
    return copies


def block_shapes(units, width):
    return [(width, units), (width, units), (units, width)]


def load_kernel(k, *refs):
    copies = fetches(k, refs[:3], refs[-4:-1], refs[-1])
    for copy in copies:
        copy.start()
    for copy in copies:
        copy.wait()


def load(k, weights, units, after=()):
    shapes = block_shapes(units, weights[0].shape[0])
    return pl.pallas_call(
        functools.partial(load_kernel, k),
        in_specs=[HOLD] * (3 + len(after)),
        out_specs=[WHOLE] * 3,
        scratch_shapes=[pltpu.SemaphoreType.DMA((FETCHES, 3))],
        out_shape=[vmem_array(x) for x in shapes],
        compiler_params=PARAMS,
        cost_estimate=estimate(0, 6 * weights[0].shape[0] * units),
        name="load",
    )(*in_hbm(weights), *after)


def sums_kernel(following, tok, grad, gate_b, up_b, down_b, *refs):
    copies = []
    if following is not None:
        hbm, out, kept, sems = refs[:3], refs[3], refs[4:7], refs[7]
        copies = fetches(following, hbm, kept, sems)
    else:
        (out,) = refs
    for copy in copies:
        copy.start()

    @pl.when(lax.axis_index("col") >= 0)
    def _():
        out[0] = dot(tok[...], gate_b[...]).astype(out.dtype)
        out[1] = dot(tok[...], up_b[...]).astype(out.dtype)
        out[2] = back_dot(grad[...], down_b[...]).astype(out.dtype)

    for copy in copies:
        copy.wait()


def partial_sums(block, tok, grad, dtype, weights=None, following=None):
    total, width = tok.shape
    units = block[2].shape[0]
    more = following is not None
    shapes = block_shapes(units, width) if more else []
    return pl.pallas_call(
        functools.partial(sums_kernel, following),
        in_specs=[WHOLE] * 5 + [HOLD] * (3 * more),
        out_specs=[WHOLE] * (1 + 3 * more),
        scratch_shapes=[pltpu.SemaphoreType.DMA((FETCHES, 3))] * more,
        out_shape=[array((3, total, units), dtype)] + [vmem_array(x) for x in shapes],
        compiler_params=PARAMS,
        cost_estimate=estimate(6 * total * width * units, 6 * width * units),
        name="partial_sums",
    )(tok, grad, *in_vmem(block), *(in_hbm(weights) if more else ()))


def combine_kernel(own, other, out, token):
    token[...] = jnp.zeros_like(token)
    out[...] = (own[...] + other[...].astype(F32)).astype(BF16)


def combine(own, other):
    return pl.pallas_call(
        combine_kernel,
        out_shape=[array(own.shape, BF16), array((8, 128), F32)],
        compiler_params=PARAMS,
        cost_estimate=estimate(own.size, 8 * own.size),
        name="combine",
    )(own, other)


def activate_kernel(own, *refs):
    others, (out, hidden, deltas) = refs[:-3], refs[-3:]
    gate, up, hidden_grad = (
        functools.reduce(lambda s, o: s + o[j].astype(F32), others, own[j]) for j in range(3)
    )
    sig = jax.nn.sigmoid(gate)
    swish = gate * sig
    out[0] = (swish * up).astype(BF16)
    out[1] = (hidden_grad * up * sig * (1.0 + gate * (1.0 - sig))).astype(BF16)
    out[2] = (hidden_grad * swish).astype(BF16)
    hidden[...] = out[0]
    deltas[...] = out[1:]


def activate(own, others):
    return pl.pallas_call(
        activate_kernel,
        out_shape=[array(x, BF16) for x in (own.shape, own.shape[1:], (2, *own.shape[1:]))],
        compiler_params=PARAMS,
        cost_estimate=estimate(8 * own.size, 12 * own.size),
        name="activate",
    )(own, *others)


def use_kernel(k, first, last, with_products, with_grads, apart, *refs):
    refs = list(refs)
    if apart:
        hidden, deltas = refs.pop(0), refs.pop(0)
        act = hidden, deltas.at[0], deltas.at[1]
    else:
        whole = refs.pop(0)
        act = whole.at[0], whole.at[1], whole.at[2]
    leaving = []
    if with_products:
        gate_w, up_w, down_w = (refs.pop(0) for _ in range(3))
        before = None if first else refs.pop(0)
    if with_grads:
        tok_t, grad = refs.pop(0), refs.pop(0)
        gate_s, up_s, down_s, sems = refs[-4:]
        refs = refs[:-4]
        gate_g, up_g, down_g = refs[-3:]
        refs = refs[:-3]
        units, width = down_s.shape
        part, rows = width // CHUNKS, units // CHUNKS
        hidden_t = act[0][...].astype(F32).T.astype(BF16)
        mine = unit_block(k, units)
        start = jnp.bitwise_xor(lax.axis_index("col"), k) * units
        for i in range(CHUNKS):
            here, some = span(i, part), span(i, rows)
            gate_s[here] = dot(tok_t[here], act[1][...]).astype(BF16)
            up_s[here] = dot(tok_t[here], act[2][...]).astype(BF16)
            down_s[some] = dot(hidden_t[some], grad[...]).astype(BF16)
            there = pl.ds(i * part, part)
            below = pl.ds(pl.multiple_of(start + i * rows, rows), rows)
            ends = (
                (gate_s.at[there], gate_g.at[there, mine]),
                (up_s.at[there], up_g.at[there, mine]),
                (down_s.at[pl.ds(i * rows, rows)], down_g.at[below]),
            )
            for j, (source, target) in enumerate(ends):
                copy = pltpu.make_async_copy(source, target, sems.at[i, j])
                copy.start()
                leaving.append(copy)
    if with_products:
        outs = refs[-1 - last :]
        for i in range(down_w.shape[1] // PIECE):
            here = span(i, PIECE)
            back = back_dot(act[1][...], gate_w[here]) + back_dot(act[2][...], up_w[here])
            for j, term in enumerate((dot(act[0][...], down_w[:, here]), back)):
                term = term if first else before[j, :, here] + term
                if last:
                    half = term.shape[0] // 2
                    outs[0][j, :, here] = term[:half]
                    outs[1][j, :, here] = term[half:]
                else:
                    outs[0][j, :, here] = term
    for copy in leaving:
        copy.wait()


def use(k, act, weights=None, terms=None, last=False, sides=None, grads=(), after=()):
    total, units = act[-1].shape[1:]
    first = terms is None
    specs, args = [WHOLE] * len(act), list(act)
    out_specs, out_shape, scratch, aliases = [], [], [], {}
    moved = 0
    if weights is not None:
        width = weights[2].shape[1]
        specs += [WHOLE] * 3
        args += in_vmem(weights)
        if not first:
            specs.append(WHOLE)
            args.append(terms)
        held = total // 2 if last else total
        out_specs += [WHOLE] * (1 + last)
        out_shape += [array((2, held, width), F32)] * (1 + last)
        moved += 6 * width * units
    if sides is not None:
        tok_t, grad, all_units = sides
        width = grad.shape[1]
        specs += [WHOLE, WHOLE]
        args += [tok_t, grad]
        for j, grad_before in enumerate(grads):
            aliases[len(args)] = len(out_shape) + j
            specs.append(HOLD)
            args.append(grad_before)
        out_specs += [HOLD] * 3
        out_shape += [pltpu.HBM((width, all_units), BF16)] * 2
        out_shape.append(pltpu.HBM((all_units, width), BF16))
        scratch += [pltpu.VMEM((width, units), BF16)] * 2
        scratch += [pltpu.VMEM((units, width), BF16), pltpu.SemaphoreType.DMA((CHUNKS, 3))]
        moved += 6 * width * units
    return pl.pallas_call(
        functools.partial(
            use_kernel, k, first, last, weights is not None, sides is not None, len(act) == 2
        ),
        in_specs=specs + [HOLD] * len(after),
        out_specs=out_specs,
        scratch_shapes=scratch,
        out_shape=out_shape,
        input_output_aliases=aliases,
        compiler_params=PARAMS,
        cost_estimate=estimate(total * moved, moved),
        name=("products" if weights else "") + ("grads" if sides else ""),
    )(*args, *after)


def fold_kernel(rows, own, other, keep, *sent):
    total = own[...] + other[...]
    keep[...] = total[:, :rows]
    for i, out in enumerate(sent, 1):
        out[...] = total[:, i * rows : (i + 1) * rows].astype(BF16)


def fold(own, other, rows):
    _, total, width = own.shape
    others = total // rows - 1
    return pl.pallas_call(
        functools.partial(fold_kernel, rows),
        out_shape=[array((2, rows, width), F32)] + [array((2, rows, width), BF16)] * others,
        compiler_params=PARAMS,
        cost_estimate=estimate(own.size, 12 * own.size),
        name="fold",
    )(own, other)


def finish_kernel(own, *refs):
    others, outs = refs[:-2], refs[-2:]
    for j, out in enumerate(outs):
        total = functools.reduce(lambda s, o: s + o[j].astype(F32), others, own[j])
        out[...] = total.astype(BF16)


def finish(own, others):
    return pl.pallas_call(
        finish_kernel,
        out_shape=[array(own.shape[1:], BF16)] * 2,
        compiler_params=PARAMS,
        cost_estimate=estimate(own.size, 12 * own.size),
        name="finish",
    )(own, *others)


def pairwise(n_row, n_col, tokens, gate_weight, up_weight, down_weight, out_grad):
    rows = tokens.shape[0]
    all_units = gate_weight.shape[1]
    units = all_units // n_col
    weights = (gate_weight, up_weight, down_weight)
    along_row = functools.partial(swap, axis="row", size=n_row)
    along_col = functools.partial(swap, axis="col", size=n_col)

    mine = pack(tokens, out_grad)
    last_weights = load(3, weights, units)
    away = [along_row(mine, k=k) for k in range(2, n_row, 2)]
    away, last_weights = lax.optimization_barrier((away, last_weights))
    even = [mine, *away]
    odd = [along_row(piece, k=1) for piece in even]
    tok, grad, tok_t = assemble(even + odd, rows)
    sides = (tok_t, grad, all_units)

    there, *near_weights = partial_sums(last_weights, tok, grad, BF16, weights, 1)
    near = along_col(there, k=1)
    there, *far_weights = partial_sums(near_weights, tok, grad, BF16, weights, 2)
    from_near = along_col(there, k=1)
    (here,) = partial_sums(far_weights, tok, grad, F32)
    pair, token = combine(here, near)
    from_far = along_col(pair, k=2)
    own_weights = load(0, weights, units, after=(token,))
    (here,) = partial_sums(own_weights, tok, grad, F32)
    own, hidden, deltas = activate(here, [from_near, from_far])

    near_act = along_col(own, k=1)
    (terms,) = use(0, (own,), own_weights)
    (hidden, deltas, own), _ = lax.optimization_barrier(((hidden, deltas, own), terms))
    far_deltas = along_col(deltas, k=2)
    far_hidden = along_col(hidden, k=2)
    grads = use(0, (own,), sides=sides)
    terms, *grads = use(1, (near_act,), near_weights, terms, sides=sides, grads=grads)
    far_deltas, _ = lax.optimization_barrier((far_deltas, (terms, grads)))
    last_deltas = along_col(far_deltas, k=1)
    far_hidden, _ = lax.optimization_barrier((far_hidden, (terms, grads)))
    last_hidden = along_col(far_hidden, k=1)
    far_act, last_act = (far_hidden, far_deltas), (last_hidden, last_deltas)
    terms, *grads = use(2, far_act, far_weights, terms, sides=sides, grads=grads)
    kept, given = use(3, last_act, last_weights, terms, last=True)

    other = along_row(given, k=1)
    mine, *sent = fold(kept, other, rows)
    parts = [along_row(piece, k=2 * i) for i, piece in enumerate(sent, 1)]
    grads = use(3, last_act, sides=sides, grads=grads, after=(mine,))
    mixed, input_grad = finish(mine, parts)
    return (mixed, input_grad, *grads)


def gathered(tokens, gate_weight, up_weight, down_weight, out_grad):
    tok = lax.all_gather(tokens, "row", axis=0, tiled=True)
    grad = lax.all_gather(out_grad, "row", axis=0, tiled=True)

    def total(x):
        return lax.psum_scatter(x, "col", scatter_dimension=0, tiled=True)

    def outer(a, b):
        return lax.dot_general(a, b, CONTRACT, preferred_element_type=F32).astype(BF16)

    gate, up = total(dot(tok, gate_weight)), total(dot(tok, up_weight))
    hidden_grad = total(back_dot(grad, down_weight))
    sig = jax.nn.sigmoid(gate)
    swish = gate * sig
    hidden = (swish * up).astype(BF16)
    gate_delta = (hidden_grad * up * sig * (1.0 + gate * (1.0 - sig))).astype(BF16)
    up_delta = (hidden_grad * swish).astype(BF16)
    hidden, gate_delta, up_delta = (
        lax.all_gather(x, "col", axis=0, tiled=True) for x in (hidden, gate_delta, up_delta)
    )
    mixed = dot(hidden, down_weight)
    input_grad = back_dot(gate_delta, gate_weight) + back_dot(up_delta, up_weight)
    mixed, input_grad = (
        lax.psum_scatter(x, "row", scatter_dimension=0, tiled=True).astype(BF16)
        for x in (mixed, input_grad)
    )
    return (
        mixed,
        input_grad,
        outer(tok, gate_delta),
        outer(tok, up_delta),
        outer(hidden, grad),
    )


def solution(mesh):
    n_row, n_col = mesh.shape["row"], mesh.shape["col"]

    def shards(*args):
        tokens, gate_weight = args[:2]
        fits = (
            n_row & (n_row - 1) == 0
            and n_row > 1
            and n_col == 4
            and tokens.shape[0] % 8 == 0
            and tokens.shape[1] % (128 * CHUNKS) == 0
            and gate_weight.shape[1] % (128 * n_col) == 0
            and gate_weight.shape[1] % (16 * CHUNKS * n_col) == 0
            and tokens.shape[1] % PIECE == 0
            and 6 * gate_weight.size <= 36 * 1024 * 1024
        )
        if fits:
            return pairwise(n_row, n_col, *args)
        return gathered(*args)

    return jax.shard_map(
        shards,
        mesh=mesh,
        in_specs=(
            P("row", "col"),
            P("col", "row"),
            P("col", "row"),
            P("row", "col"),
            P("row", "col"),
        ),
        out_specs=(
            P("row", "col"),
            P("row", "col"),
            P("col", "row"),
            P("col", "row"),
            P("row", "col"),
        ),
        check_vma=False,
    )
```
